32 devices in a mesh: grp: 2 (over core), dev: 16 (over z, y, x).
Axes of the slice: x: 2, y: 2, z: 4, core: 2. Of those that a mesh axis runs over, the one named last changes fastest.
Arguments:
- residual_in: bfloat16 [512, 2048], P(('grp', 'dev')), may hold values from -1.5 to 1.5
- queries: bfloat16 [2, 256, 4096], P(None, 'dev', 'grp'), may hold values from -2.5 to 2.5
- latest_key_value: bfloat16 [2, 256, 4, 256], P(None, 'dev', 'grp'), may hold values from -2.5 to 2.5
- key_value_cache: bfloat16 [2, 256, 4, 256, 256], P(None, 'dev', 'grp'), may hold values from -2.5 to 2.5
- cache_len: int32 [2, 256], P(None, 'dev'), may hold values from 1 to 256, 32768 in all within a row
- out_weight: bfloat16 [4096, 2048], P('grp'), may hold values from -0.09375 to 0.09375
- norm_gain: bfloat16 [2048], replicated, may hold values from 0.099609375 to 1.8984375
- router_weight: bfloat16 [2048, 32], replicated, may hold values from -0.125 to 0.125
- routes: int32 [512, 8], P(('grp', 'dev')), may hold values from 0 to 31, all different within a row; in each aligned block of 16 rows (0 to 15, 16 to 31, ...) at most 8 rows name the same one
- expert_gate_up: bfloat16 [32, 2048, 1536], P(('grp', 'dev')), may hold values from -0.125 to 0.125
- expert_down: bfloat16 [32, 768, 2048], P(('grp', 'dev')), may hold values from -0.21875 to 0.21875
Outputs:
- layer_out: bfloat16 [512, 2048], P(('grp', 'dev'))
The draws below stay inside these ranges and needn't reach their ends.
Inputs may be any that keep to these rules, and one draw needn't show every extreme that they name: Each row of cache_len of 256 entries sums to 32768, and its largest entry is exactly 256. `routes`: the 8 experts of a row are distinct; in each aligned block of 16 rows (the rows of one device) no expert is named by more than 8 rows, a bound that some block reaches.
All inputs are finite; a program needn't handle non-finite values. No bound on the sum of `cache_len` on one device may be relied on, other than what follows from the above.
Results may differ from the reference program's by a relative error of at most 0.017.
Values may be sent and summed in bfloat16 or wider, within the bound.
A program may use at most 128 MiB of HBM per device.

```python
import math
import jax
import jax.numpy as jnp
import numpy as np
from jax import lax

D = 2048
QUERY_HEADS = 32
KEY_VALUE_HEADS = 4
HEAD_SIZE = 128
FF = 768
TOPK = 8
CACHE_SLOTS_MAX = 256
TOK = 16
EXPERTS = 32
HALF_BATCH_ROWS = 256
ROWS = 512
CAP = 8


def block_levels(rng, dims, split, smallest, top_value):
    def one(dim, shards_of):
        heights = jax.random.uniform(jax.random.fold_in(jax.random.fold_in(rng, 6), dim), (shards_of,), jnp.float32, smallest / len(split), top_value / len(split))
        return jnp.repeat(jnp.exp(heights), dims[dim] // shards_of).reshape((-1,) + (1,) * (len(dims) - dim - 1))

    factor_of = one(*split[0])
    for cut in split[1:]:
        factor_of = factor_of * one(*cut)
    return factor_of


def profile(count, total, most, lean):
    portions = [(1 << 20) // math.isqrt(standing ** lean) + 1 for standing in range(2, count + 1)]
    spare, holding = total - most - (count - 1), [1] * (count - 1)
    while spare > 0:
        movable = [i for i in range(count - 1) if holding[i] < most]
        whole, budget = sum([portions[i] for i in movable]), spare
        for i in movable:
            more = min(most - holding[i], max(1, budget * portions[i] // whole), spare)
            holding[i] = holding[i] + more
            spare = spare - more
    return np.array([most] + holding)


def uneven_parts(key, amount, total, bound, lean):
    if amount == 2:
        one = jax.random.randint(key, (), max(1, total - bound), min(bound, total - 1) + 1)
        return jnp.stack([one, total - one])
    sizes = jnp.asarray(profile(amount, total, bound, lean), jnp.int32)
    pairs = (amount - 1) // 2
    giver, taker = sizes[1:1 + 2 * pairs:2], sizes[2:2 + 2 * pairs:2]
    margin = jnp.minimum(giver - 1, bound - taker)
    passed = jax.random.randint(jax.random.fold_in(key, 1), (pairs,), 0, 1 << 20) % (margin + 1)
    sizes = sizes.at[1:1 + 2 * pairs:2].set(giver - passed).at[2:2 + 2 * pairs:2].set(taker + passed)
    return sizes[jax.random.permutation(jax.random.fold_in(key, 2), amount)]


def assign_block(key, own, number, rows, amount, top, reach, skew):
    sequence = jax.random.permutation(key, amount)
    heavy_load, common = load_shares(amount, rows * top, reach, skew, True), load_shares(amount, rows * top, reach, skew, False)
    places = jnp.arange(amount)

    def named(sizes, offset_by):
        used = int((sizes > 0).sum())
        fixed = max(1, used // 4)
        moved = fixed + (places - fixed + offset_by * (used - fixed)) % max(1, amount - fixed)
        return jnp.zeros((amount,), jnp.int32).at[sequence[jnp.where(places < fixed, places, moved)]].set(jnp.asarray(sizes, jnp.int32))

    sizes = jnp.where(number % 4 == 0, named(heavy_load, number // 4), named(common, number - number // 4 - 1))
    mixed = jax.random.permutation(jax.random.fold_in(own, 3), amount)
    donor, receiver = mixed[0:amount // 2 * 2:2], mixed[1:amount // 2 * 2:2]
    room = jnp.minimum(sizes[donor] - 1, reach - sizes[receiver]) // 2
    room = jnp.where((donor == sequence[0]) | (receiver == sequence[0]) | (sizes[receiver] == 0), 0, jnp.maximum(room, 0))
    moved = jax.random.randint(jax.random.fold_in(own, 4), (amount // 2,), 0, 1 << 20) % (room + 1)
    sizes = sizes.at[donor].add(-moved).at[receiver].add(moved)
    items = jnp.searchsorted(jnp.cumsum(sizes), jnp.arange(rows * top), side="right").astype(jnp.int32)
    table = items.reshape(top, rows).T
    table = table[jax.random.permutation(jax.random.fold_in(own, 1), rows)]
    offset_by = jax.random.randint(jax.random.fold_in(own, 2), (rows, 1), 0, top)
    return jnp.take_along_axis(table, (jnp.arange(top)[None, :] + offset_by) % top, axis=1)


def load_shares(count, total, limit, skew, full):
    loads = [(1 << 20) // math.isqrt(standing ** skew) + 1 for standing in range(1, count + 1)]
    largest = limit if full else min(limit, max(-(-total // count), total * loads[0] // sum(loads)))
    least = 1 if total - largest >= count - 1 else 0
    holding, spare = [largest] + [least] * (count - 1), total - largest - least * (count - 1)
    while spare > 0:
        movable = [i for i in range(1, count) if holding[i] < largest] or [i for i in range(1, count) if holding[i] < limit]
        pool, remaining = sum([loads[i] for i in movable]), spare
        for i in movable:
            more = min(limit - holding[i], max(1, remaining * loads[i] // pool), spare)
            holding[i] = holding[i] + more
            spare = spare - more
    return np.array(holding)


def gaussian(stream_key, extent, spread, bound, shards=(), kind=jnp.bfloat16):
    array = jax.random.normal(stream_key, extent, jnp.float32) * spread
    if len(shards) > 0:
        array = block_levels(stream_key, extent, shards, -0.22, 0.18) * array
    return jnp.clip(array, min=-bound, max=bound).astype(kind)


def setup_inputs(seed: int = 0) -> dict:
    streams_of = jax.random.split(jax.random.key(seed), 12)
    residual_in = gaussian(streams_of[0], (ROWS, D), 0.1, 1.5, ((0, 32),))
    queries = gaussian(streams_of[1], (2, HALF_BATCH_ROWS, QUERY_HEADS * HEAD_SIZE), 1.0, 2.5, ((1, 16), (2, 2)))
    latest_key_value = gaussian(streams_of[2], (2, HALF_BATCH_ROWS, KEY_VALUE_HEADS, 2 * HEAD_SIZE), 1.0, 2.5, ((1, 16), (2, 2)))
    key_value_cache = gaussian(streams_of[3], (2, HALF_BATCH_ROWS, KEY_VALUE_HEADS, CACHE_SLOTS_MAX, 2 * HEAD_SIZE), 1.0, 2.5, ((1, 16), (2, 2)))
    cache_len = jax.vmap(lambda own: uneven_parts(own, HALF_BATCH_ROWS, HALF_BATCH_ROWS * CACHE_SLOTS_MAX // 2, CACHE_SLOTS_MAX, 2))(jax.random.split(streams_of[4], 2)).reshape((2, HALF_BATCH_ROWS)).astype(jnp.int32)
    out_weight = gaussian(streams_of[5], (QUERY_HEADS * HEAD_SIZE, D), (QUERY_HEADS * HEAD_SIZE) ** -0.5, 0.09375, ((0, 2),))
    norm_gain = jnp.clip(1.0 + 0.18 * jax.random.normal(streams_of[6], (D,), jnp.float32), 0.099609375, 1.8984375).astype(jnp.bfloat16)
    router_weight = gaussian(streams_of[7], (D, EXPERTS), D ** -0.5, 0.125)
    routes_keys = jax.random.split(jax.random.fold_in(streams_of[8], 1), ROWS // TOK)
    routes_turns = jax.random.permutation(jax.random.fold_in(streams_of[8], 3), ROWS // TOK)
    routes = jax.vmap(lambda own, number: assign_block(jax.random.fold_in(streams_of[8], 2), own, number, TOK, EXPERTS, TOPK, CAP, 2))(routes_keys, routes_turns).reshape((ROWS, TOPK))
    expert_gate_up = gaussian(streams_of[9], (EXPERTS, D, 2 * FF), D ** -0.5, 0.125, ((0, 32),))
    expert_down = gaussian(streams_of[10], (EXPERTS, FF, D), FF ** -0.5, 0.21875, ((0, 32),))
    return dict(residual_in=residual_in, queries=queries, latest_key_value=latest_key_value, key_value_cache=key_value_cache, cache_len=cache_len, out_weight=out_weight, norm_gain=norm_gain, router_weight=router_weight, routes=routes, expert_gate_up=expert_gate_up, expert_down=expert_down)


def attend_half(query_vector, fresh, cache, lengths):
    batch_rows = query_vector.shape[0]
    query_group = QUERY_HEADS // KEY_VALUE_HEADS
    query_stack = query_vector.astype(jnp.float32).reshape(batch_rows, KEY_VALUE_HEADS, query_group, HEAD_SIZE)
    scale = 1.0 / math.sqrt(HEAD_SIZE)
    visible = jnp.arange(CACHE_SLOTS_MAX, dtype=jnp.int32)[None, None, :] < lengths[:, None, None]

    def single_head(head):
        cache_head = lax.dynamic_index_in_dim(cache, head, 1, keepdims=False).astype(jnp.float32)
        fresh_head = lax.dynamic_index_in_dim(fresh, head, 1, keepdims=False).astype(jnp.float32)
        query_head = lax.dynamic_index_in_dim(query_stack, head, 1, keepdims=False)
        scores = jnp.einsum('rgd,rsd->rgs', query_head, cache_head[:, :, :HEAD_SIZE]) * scale
        own_score = jnp.einsum('rgd,rd->rg', query_head, fresh_head[:, :HEAD_SIZE]) * scale
        raised = jnp.where(visible, jnp.exp(scores), 0.0)
        own_raised = jnp.exp(own_score)
        totals = lax.optimization_barrier(jnp.sum(raised, axis=-1)) + own_raised
        weights = lax.optimization_barrier((raised / totals[:, :, None]).astype(jnp.bfloat16)).astype(jnp.float32)
        own_weight = lax.optimization_barrier((own_raised / totals).astype(jnp.bfloat16)).astype(jnp.float32)
        mixed = jnp.einsum('rgs,rsd->rgd', weights, cache_head[:, :, HEAD_SIZE:])
        return mixed + own_weight[:, :, None] * fresh_head[:, None, HEAD_SIZE:]
    head_list = lax.map(single_head, jnp.arange(KEY_VALUE_HEADS, dtype=jnp.int32))
    return jnp.transpose(head_list, (1, 0, 2, 3)).reshape(batch_rows, QUERY_HEADS * HEAD_SIZE).astype(jnp.bfloat16)

def reference(residual_in, queries, latest_key_value, key_value_cache, cache_len, out_weight, norm_gain, router_weight, routes, expert_gate_up, expert_down):
    attended = jnp.concatenate([attend_half(queries[index], latest_key_value[index], key_value_cache[index], cache_len[index]) for index in range(2)], axis=0)
    projected = jnp.dot(attended, out_weight, preferred_element_type=jnp.float32)
    hidden = residual_in.astype(jnp.float32) + projected
    meansq = lax.optimization_barrier(jnp.mean(hidden * hidden, axis=-1, keepdims=True))
    normed = (hidden * lax.rsqrt(meansq + 1e-06) * norm_gain.astype(jnp.float32)).astype(jnp.bfloat16)
    logits = jnp.dot(normed, router_weight, preferred_element_type=jnp.float32)
    picked = jnp.exp(jnp.take_along_axis(logits, routes, axis=1))
    gates = picked / lax.optimization_barrier(jnp.sum(picked, axis=1, keepdims=True))
    sources = ROWS // TOK
    assigned = TOK * TOPK
    flat_routes = routes.reshape(sources, assigned)
    onehot = (flat_routes[:, :, None] == jnp.arange(EXPERTS, dtype=jnp.int32)[None, None, :]).astype(jnp.int32)
    ranks = lax.optimization_barrier(jnp.sum(onehot * (jnp.cumsum(onehot, axis=1) - 1), axis=2)).astype(jnp.int32)
    target = (flat_routes * CAP + ranks).astype(jnp.int32)
    repeated = jnp.repeat(normed.reshape(sources, TOK, D), TOPK, axis=1)

    def place(targets, values):
        return jnp.zeros((EXPERTS * CAP, D), jnp.bfloat16).at[targets].set(values)
    slots = jax.vmap(place)(target, repeated).reshape(sources, EXPERTS, CAP, D)

    def one_expert(expert):
        inputs = lax.dynamic_index_in_dim(slots, expert, 1, keepdims=False).reshape(sources * CAP, D)
        weight_in = lax.dynamic_index_in_dim(expert_gate_up, expert, 0, keepdims=False)
        weight_out = lax.dynamic_index_in_dim(expert_down, expert, 0, keepdims=False)
        gate_up = jnp.dot(inputs, weight_in, preferred_element_type=jnp.float32)
        active = (jax.nn.silu(gate_up[:, :FF]) * gate_up[:, FF:]).astype(jnp.bfloat16)
        result = jnp.dot(active, weight_out, preferred_element_type=jnp.float32).astype(jnp.bfloat16)
        return result.reshape(sources, CAP, D)
    served = lax.map(one_expert, jnp.arange(EXPERTS, dtype=jnp.int32))
    returned = jnp.transpose(served, (1, 0, 2, 3)).reshape(sources, EXPERTS * CAP, D)
    picked_rows = jax.vmap(lambda table, position: table[position])(returned, target)
    picked_rows = picked_rows.reshape(ROWS, TOPK, D).astype(jnp.float32)
    combined = lax.optimization_barrier(jnp.sum(gates[:, :, None] * picked_rows, axis=1))
    return (hidden + combined).astype(jnp.bfloat16)
```

```python
import functools
import math

import jax
import jax.numpy as jnp
from jax import lax
from jax.experimental import pallas as pl
from jax.experimental.pallas import tpu as pltpu
from jax.sharding import PartitionSpec as P

HEAD_SIZE = 128
MESH = pl.DeviceIdType.MESH
ROWS_STEP = 8
VMEM_LIMIT = 56 * 1024 * 1024


def attend_kernel(steps, lens_ref, q_ref, new_ref, cache_ref, wo_hbm, out_ref, att, wo, sem):
    i = pl.program_id(0)
    rows, kv_heads, positions, _ = cache_ref.shape
    q_heads = q_ref.shape[1] // HEAD_SIZE
    group = q_heads // kv_heads
    scale = 1.0 / math.sqrt(HEAD_SIZE)

    @pl.when(i == 0)
    def _():
        pltpu.make_async_copy(wo_hbm, wo, sem).start()

    q = q_ref[...].astype(jnp.float32)
    q = jnp.stack([q[:, j * HEAD_SIZE : (j + 1) * HEAD_SIZE] for j in range(q_heads)], axis=0)
    q = jnp.swapaxes(q, 0, 1)
    new = new_ref[...].astype(jnp.float32)
    place = lax.broadcasted_iota(jnp.int32, (group, positions), 1)
    mixed = []
    for r in range(rows):
        length = lens_ref[i * rows + r]
        heads = []
        for h in range(kv_heads):
            qh = q[r, h * group : (h + 1) * group]
            s = lax.dot_general(
                qh.astype(jnp.bfloat16),
                cache_ref[r, h, :, :HEAD_SIZE],
                (((1,), (1,)), ((), ())),
                preferred_element_type=jnp.float32,
            )
            e = jnp.where(place < length, jnp.exp(s * scale), 0.0)
            fresh = new[r, h : h + 1]
            own = jnp.exp(jnp.sum(qh * fresh[:, :HEAD_SIZE], axis=1, keepdims=True) * scale)
            total = jnp.sum(e, axis=1, keepdims=True) + own
            w = (e / total).astype(jnp.bfloat16)
            own_w = (own / total).astype(jnp.bfloat16).astype(jnp.float32)
            o = jnp.dot(w, cache_ref[r, h, :, HEAD_SIZE:], preferred_element_type=jnp.float32)
            heads.append(o + own_w * fresh[:, HEAD_SIZE:])
        mixed.append(jnp.concatenate(heads, axis=0))
    mixed = jnp.swapaxes(jnp.stack(mixed, axis=0), 0, 1)
    att[i] = jnp.concatenate([mixed[j] for j in range(q_heads)], axis=1)

    @pl.when(i == steps - 1)
    def _():
        pltpu.make_async_copy(wo_hbm, wo, sem).wait()
        a = att[...].reshape(steps * rows, q_heads * HEAD_SIZE).astype(jnp.bfloat16)
        out_ref[...] = jnp.dot(a, wo[...], preferred_element_type=jnp.float32)


def attend(queries, latest, cache, lens, out_weight):
    total, q_width = queries.shape
    kv_heads, positions, kv_width = cache.shape[1:]
    width = out_weight.shape[1]
    steps = total // ROWS_STEP
    return pl.pallas_call(
        functools.partial(attend_kernel, steps),
        grid=(steps,),
        out_shape=jax.ShapeDtypeStruct((total, width), jnp.float32),
        in_specs=[
            pl.BlockSpec(memory_space=pltpu.SMEM),
            pl.BlockSpec((ROWS_STEP, q_width), lambda i: (i, 0)),
            pl.BlockSpec((ROWS_STEP, kv_heads, kv_width), lambda i: (i, 0, 0)),
            pl.BlockSpec((ROWS_STEP, kv_heads, positions, kv_width), lambda i: (i, 0, 0, 0)),
            pl.BlockSpec(memory_space=pl.ANY),
        ],
        out_specs=pl.BlockSpec((total, width), lambda i: (0, 0)),
        scratch_shapes=[
            pltpu.VMEM((steps, ROWS_STEP, q_width), jnp.float32),
            pltpu.VMEM(out_weight.shape, out_weight.dtype),
            pltpu.SemaphoreType.DMA,
        ],
        compiler_params=pltpu.CompilerParams(vmem_limit_bytes=VMEM_LIMIT),
        name="attend",
    )(lens, queries, latest, cache, out_weight)


def moe_kernel(
    n,
    bits,
    partial_ref,
    res_ref,
    gain_ref,
    router_ref,
    routes_ref,
    wgu_hbm,
    wd_hbm,
    out_ref,
    wgu,
    wd,
    xsib,
    hid,
    gath,
    act,
    part,
    rsib,
    racc,
    wsem,
    xsem,
    gsend,
    grecv,
    ssend,
    srecv,
    bsend,
    brecv,
    rsend,
    rrecv,
):
    g = lax.axis_index("grp")
    d = lax.axis_index("dev")
    tok, width = res_ref.shape
    experts = router_ref.shape[1]
    ff = wd.shape[0]
    sib = (1 - g, d)

    def peer(j):
        m = 1 << (bits - 1 - j)
        if bits >= 2 and j == bits - 2:
            m = 1 + g
        elif bits >= 2 and j == bits - 1:
            m = 2 - g
        return (g, d + m * (1 - 2 * ((d // m) % 2)))

    peers = [peer(j) for j in range(bits)]
    load_gu = pltpu.make_async_copy(wgu_hbm.at[0], wgu, wsem.at[0])
    load_d = pltpu.make_async_copy(wd_hbm.at[0], wd, wsem.at[1])
    load_gu.start()
    load_d.start()

    barrier = pltpu.get_barrier_semaphore()
    for target in peers + [sib]:
        pl.semaphore_signal(barrier, inc=1, device_id=target, device_id_type=MESH)
    pl.semaphore_wait(barrier, bits + 1)

    def remote(src, dst, send, recv, target):
        return pltpu.make_async_remote_copy(
            src_ref=src,
            dst_ref=dst,
            send_sem=send,
            recv_sem=recv,
            device_id=target,
            device_id_type=MESH,
        )

    swap = remote(partial_ref.at[1 - g], xsib, xsem.at[0], xsem.at[1], sib)
    swap.start()
    swap.wait()
    hidden = res_ref[...].astype(jnp.float32) + (partial_ref[g] + xsib[...])
    hid[...] = hidden
    meansq = jnp.mean(hidden * hidden, axis=-1, keepdims=True)
    normed = (hidden * lax.rsqrt(meansq + 1e-06) * gain_ref[...].astype(jnp.float32)).astype(
        jnp.bfloat16
    )
    logits = jnp.dot(normed, router_ref[...], preferred_element_type=jnp.float32)
    lane = lax.broadcasted_iota(jnp.int32, (tok, experts), 1)
    routes = routes_ref[...]
    routed = lane == routes[:, 0:1]
    for k in range(1, routes.shape[1]):
        routed = jnp.logical_or(routed, lane == routes[:, k : k + 1])
    picked = jnp.where(routed, jnp.exp(logits), 0.0)
    gates = picked / jnp.sum(picked, axis=1, keepdims=True)
    extra = gath.shape[3] - width
    if extra > experts:
        gates = jnp.concatenate([gates, jnp.zeros((tok, extra - experts), jnp.float32)], axis=1)
    gath[0, 0, :, :width] = normed
    gath[0, 0, :, width:] = gates.astype(jnp.bfloat16)

    sends = []

    def forward(slot):
        first = slot.bit_length()
        for j in range(bits - 1, first - 1, -1):
            there = slot | (1 << j)
            sends.append(
                remote(gath.at[0, slot], gath.at[0, there], gsend.at[there], grecv.at[there], peers[j])
            )
            sends[-1].start()
        sends.append(remote(gath.at[0, slot], gath.at[1, slot], ssend.at[slot], srecv.at[slot], sib))
        sends[-1].start()

    def arrived(slot):
        remote(gath.at[0, slot], gath.at[0, slot], gsend.at[slot], grecv.at[slot], sib).wait_recv()

    def arrived_sib(slot):
        remote(gath.at[0, slot], gath.at[1, slot], ssend.at[slot], srecv.at[slot], sib).wait_recv()

    half = n // 2
    forward(0)
    for slot in range(1, half):
        arrived(slot)
        forward(slot)

    expert = g * n + d
    group = min(8, half)
    rows = 2 * group * tok

    def gate_up(base, t, tile):
        x = gath[:, pl.ds(base, group), :, :width].reshape(rows, width)
        gate = jnp.dot(x, wgu[:, t : t + tile], preferred_element_type=jnp.float32)
        up = jnp.dot(x, wgu[:, ff + t : ff + t + tile], preferred_element_type=jnp.float32)
        act[:, t : t + tile] = (gate / (1.0 + jnp.exp(-gate)) * up).astype(jnp.bfloat16)

    def down(base):
        weights = gath[:, pl.ds(base, group), :, width:].reshape(rows, extra).astype(jnp.float32)
        mine = lax.broadcasted_iota(jnp.int32, (rows, extra), 1) == expert
        weight = jnp.sum(jnp.where(mine, weights, 0.0), axis=1, keepdims=True)
        tile = 512
        for t in range(0, width, tile):
            y = jnp.dot(act[...], wd[:, t : t + tile], preferred_element_type=jnp.float32)
            y = (y * weight).astype(jnp.bfloat16).reshape(2, group, tok, tile)
            part[:, pl.ds(base, group), :, t : t + tile] = y

    FT = 256
    for slot in range(half):
        arrived_sib(slot)
    load_gu.wait()
    pending = list(range(half, n))
    tiles = list(range(0, ff, FT))
    for at in range(0, half, group):
        for t in tiles:
            gate_up(at, t, FT)
            if at == 0:
                count = -(-half // len(tiles))
                for slot in pending[:count]:
                    arrived(slot)
                    forward(slot)
                pending = pending[count:]
        if at == 0:
            load_d.wait()
        down(at)

    def give(slot):
        sends.append(remote(part.at[1, slot], rsib.at[slot], bsend.at[slot], brecv.at[slot], sib))
        sends[-1].start()

    def taken(slot):
        remote(part.at[1, slot], rsib.at[slot], bsend.at[slot], brecv.at[slot], sib).wait_recv()
        part[0, slot] = (
            part[0, slot].astype(jnp.float32) + rsib[slot].astype(jnp.float32)
        ).astype(jnp.bfloat16)

    order = [bits - 2, bits - 1] + list(range(bits - 3, -1, -1)) if bits >= 2 else [0]

    def ship(slot, step):
        j = order[step]
        there = slot ^ (1 << j)
        sends.append(
            remote(part.at[0, slot], racc.at[slot], rsend.at[slot], rrecv.at[slot], peers[j])
        )
        sends[-1].start()

    def absorb(slot, step):
        j = order[step]
        source = slot | (1 << j)
        remote(part.at[0, slot], racc.at[source], rsend.at[source], rrecv.at[source], sib).wait_recv()
        part[0, slot] = (
            part[0, slot].astype(jnp.float32) + racc[source].astype(jnp.float32)
        ).astype(jnp.bfloat16)

    for slot in range(half):
        give(slot)
    for slot in range(half, n):
        arrived_sib(slot)
    for at in range(half, n, group):
        for t in tiles:
            gate_up(at, t, FT)
            if at == half and t == tiles[0]:
                for slot in range(half):
                    taken(slot)
                    if slot & (1 << order[0]):
                        ship(slot, 0)
        down(at)
    for slot in range(half, n):
        give(slot)
    for slot in reversed(range(half, n)):
        taken(slot)
        if slot & (1 << order[0]):
            ship(slot, 0)

    live = [s for s in range(n) if not s & (1 << order[0])]
    for step in range(1, len(order)):
        j = order[step]
        out_going = [s for s in live if s & (1 << j)]
        staying = [s for s in live if not s & (1 << j)]
        for s in out_going:
            absorb(s, step - 1)
            ship(s, step)
        for s in staying:
            absorb(s, step - 1)
        live = staying
    source = 1 << order[-1]
    remote(part.at[0, 0], racc.at[source], rsend.at[source], rrecv.at[source], sib).wait_recv()
    out_ref[...] = (
        hid[...] + (part[0, 0].astype(jnp.float32) + racc[source].astype(jnp.float32))
    ).astype(jnp.bfloat16)
    for copy in sends:
        copy.wait_send()


def moe(n, partial, residual, gain, router, routes, gate_up, down):
    tok, width = residual.shape
    bits = n.bit_length() - 1
    extra = -(-router.shape[1] // 128) * 128
    group = min(8, n // 2)
    bf16 = jnp.bfloat16
    dma = pltpu.SemaphoreType.DMA
    vmem = pl.BlockSpec(memory_space=pltpu.VMEM)
    hbm = pl.BlockSpec(memory_space=pl.ANY)
    return pl.pallas_call(
        functools.partial(moe_kernel, n, bits),
        out_shape=jax.ShapeDtypeStruct((tok, width), bf16),
        in_specs=[vmem] * 5 + [hbm] * 2,
        out_specs=vmem,
        scratch_shapes=[
            pltpu.VMEM(gate_up.shape[1:], bf16),
            pltpu.VMEM(down.shape[1:], bf16),
            pltpu.VMEM((tok, width), jnp.float32),
            pltpu.VMEM((tok, width), jnp.float32),
            pltpu.VMEM((2, n, tok, width + extra), bf16),
            pltpu.VMEM((2 * group * tok, down.shape[1]), bf16),
            pltpu.VMEM((2, n, tok, width), bf16),
            pltpu.VMEM((n, tok, width), bf16),
            pltpu.VMEM((n, tok, width), bf16),
            dma((2,)),
            dma((2,)),
            dma((n,)),
            dma((n,)),
            dma((n,)),
            dma((n,)),
            dma((n,)),
            dma((n,)),
            dma((n,)),
            dma((n,)),
        ],
        compiler_params=pltpu.CompilerParams(
            collective_id=0, has_side_effects=True, vmem_limit_bytes=VMEM_LIMIT
        ),
        name="moe",
    )(partial, residual, gain, router, routes, gate_up, down)


def solution(mesh):
    n = mesh.shape["dev"]

    def per_device(
        residual_in,
        queries,
        latest_key_value,
        key_value_cache,
        cache_len,
        out_weight,
        norm_gain,
        router_weight,
        routes,
        expert_gate_up,
        expert_down,
    ):
        halves, tokens = queries.shape[:2]
        total = halves * tokens
        partial = attend(
            queries.reshape(total, -1),
            latest_key_value.reshape((total,) + latest_key_value.shape[2:]),
            key_value_cache.reshape((total,) + key_value_cache.shape[2:]),
            cache_len.reshape(total),
            out_weight,
        )
        return moe(
            n,
            partial.reshape(halves, tokens, -1),
            residual_in,
            norm_gain.reshape(1, -1),
            router_weight,
            routes,
            expert_gate_up,
            expert_down,
        )

    placed = (
        P(("grp", "dev"), None),
        P(None, "dev", "grp"),
        P(None, "dev", "grp", None),
        P(None, "dev", "grp", None, None),
        P(None, "dev"),
        P("grp", None),
        P(),
        P(),
        P(("grp", "dev"), None),
        P(("grp", "dev"), None, None),
        P(("grp", "dev"), None, None),
    )
    return jax.shard_map(
        per_device, mesh=mesh, in_specs=placed, out_specs=P(("grp", "dev"), None), check_vma=False
    )
```

```python
import functools
import math

import jax
import jax.numpy as jnp
from jax import lax
from jax.experimental import pallas as pl
from jax.experimental.pallas import tpu as pltpu
from jax.sharding import PartitionSpec as P

HEAD_SIZE = 128
MESH = pl.DeviceIdType.MESH
ROWS_STEP = 8
OUT_TILE = 512
VMEM_LIMIT = 60 * 1024 * 1024


def layer_kernel(
    n,
    bits,
    lens_ref,
    q_ref,
    new_ref,
    cache_hbm,
    wo_hbm,
    res_ref,
    gain_ref,
    router_ref,
    routes_ref,
    wgu_hbm,
    wd_hbm,
    out_ref,
    kv,
    wo,
    wgu,
    wd,
    qs,
    att,
    pout,
    xsib,
    hid,
    gath,
    act,
    part,
    rsib,
    racc,
    ksem,
    wsem,
    xsend,
    xrecv,
    gsend,
    grecv,
    ssend,
    srecv,
    bsend,
    brecv,
    rsend,
    rrecv,
):
    g = lax.axis_index("grp")
    d = lax.axis_index("dev")
    tok, width = res_ref.shape
    experts = router_ref.shape[0]
    ff = wd.shape[0]
    sib = (1 - g, d)
    halves, tokens = q_ref.shape[:2]
    per_half = tokens // ROWS_STEP
    steps = halves * per_half
    kv_heads, positions = cache_hbm.shape[2:4]
    q_heads = q_ref.shape[2] // HEAD_SIZE
    group = q_heads // kv_heads
    scale = 1.0 / math.sqrt(HEAD_SIZE)

    def load_kv(half, s):
        return pltpu.make_async_copy(
            cache_hbm.at[half, pl.ds(s * ROWS_STEP, ROWS_STEP)],
            kv.at[half, s],
            ksem.at[half, s],
        )

    load_o = pltpu.make_async_copy(wo_hbm, wo, wsem.at[0])
    load_gu = pltpu.make_async_copy(wgu_hbm.at[0], wgu, wsem.at[1])
    load_d = pltpu.make_async_copy(wd_hbm.at[0], wd, wsem.at[2])
    for half in range(halves):
        for s in range(per_half):
            load_kv(half, s).start()

    def peer(j):
        m = 1 << (bits - 1 - j)
        if bits >= 2 and j == bits - 2:
            m = 1 + g
        elif bits >= 2 and j == bits - 1:
            m = 2 - g
        return (g, d + m * (1 - 2 * ((d // m) % 2)))

    peers = [peer(j) for j in range(bits)]
    barrier = pltpu.get_barrier_semaphore()
    for target in peers + [sib]:
        pl.semaphore_signal(barrier, inc=1, device_id=target, device_id_type=MESH)

    def remote(src, dst, send, recv, target):
        return pltpu.make_async_remote_copy(
            src_ref=src,
            dst_ref=dst,
            send_sem=send,
            recv_sem=recv,
            device_id=target,
            device_id_type=MESH,
        )

    for half in range(halves):
        q = q_ref[half].astype(jnp.float32)
        q = jnp.stack([q[:, j * HEAD_SIZE : (j + 1) * HEAD_SIZE] for j in range(q_heads)], axis=0)
        qs[half] = jnp.swapaxes(q, 0, 1)

    pairs = [(r, h) for r in range(ROWS_STEP) for h in range(kv_heads)]

    def attend(i, carry):
        half = i // per_half
        s = i % per_half
        load_kv(half, s).wait()

        @pl.when(i == 0)
        def _():
            load_o.start()

        first = pl.multiple_of(s * ROWS_STEP, ROWS_STEP)
        q = qs[half, pl.ds(first, ROWS_STEP)].reshape(ROWS_STEP, kv_heads, group, HEAD_SIZE)
        new = new_ref[half, pl.ds(first, ROWS_STEP)].astype(jnp.float32)[:, :, None, :]
        own = jnp.exp(jnp.sum(q * new[..., :HEAD_SIZE], axis=-1, keepdims=True) * scale)
        qb = q.astype(jnp.bfloat16)
        place = lax.broadcasted_iota(jnp.int32, (group, positions), 1)
        lens = [lens_ref[half, first + r] for r in range(ROWS_STEP)]
        scores = [
            lax.dot_general(
                qb[r, h],
                kv[half, s, r, h, :, :HEAD_SIZE],
                (((1,), (1,)), ((), ())),
                preferred_element_type=jnp.float32,
            )
            for r, h in pairs
        ]
        raised = [
            jnp.where(place < lens[r], jnp.exp(x * scale), 0.0) for (r, h), x in zip(pairs, scores)
        ]
        inverse = [
            1.0 / (jnp.sum(e, axis=1, keepdims=True) + own[r, h]) for (r, h), e in zip(pairs, raised)
        ]
        weights = [(e * v).astype(jnp.bfloat16) for e, v in zip(raised, inverse)]
        mixed = [
            jnp.dot(w, kv[half, s, r, h, :, HEAD_SIZE:], preferred_element_type=jnp.float32)
            for (r, h), w in zip(pairs, weights)
        ]
        mixed = [
            o
            + (own[r, h] * v).astype(jnp.bfloat16).astype(jnp.float32) * new[r, h, :, HEAD_SIZE:]
            for (r, h), o, v in zip(pairs, mixed, inverse)
        ]
        mixed = jnp.stack(
            [
                jnp.concatenate(mixed[r * kv_heads : (r + 1) * kv_heads], axis=0)
                for r in range(ROWS_STEP)
            ],
            axis=0,
        )
        mixed = jnp.swapaxes(mixed, 0, 1)
        att[i] = jnp.concatenate([mixed[j] for j in range(q_heads)], axis=1)
        return carry

    lax.fori_loop(0, steps, attend, 0)
    load_gu.start()
    load_d.start()
    pl.semaphore_wait(barrier, bits + 1)
    load_o.wait()
    attended = att[...].reshape(halves * tokens, q_heads * HEAD_SIZE).astype(jnp.bfloat16)
    swaps = []
    for t in range(width // OUT_TILE):
        cols = slice(t * OUT_TILE, (t + 1) * OUT_TILE)
        y = jnp.dot(attended, wo[:, cols], preferred_element_type=jnp.float32)
        pout[t] = y.reshape(halves, tokens, OUT_TILE)
        swaps.append(remote(pout.at[t, 1 - g], xsib.at[t], xsend.at[t], xrecv.at[t], sib))
        swaps[-1].start()
    squares = jnp.zeros((tok, 1), jnp.float32)
    for t in range(width // OUT_TILE):
        cols = slice(t * OUT_TILE, (t + 1) * OUT_TILE)
        swaps[t].wait()
        h = res_ref[:, cols].astype(jnp.float32) + (pout[t, g] + xsib[t])
        hid[:, cols] = h
        squares = squares + jnp.sum(h * h, axis=-1, keepdims=True)
    inv_norm = lax.rsqrt(squares * (1.0 / width) + 1e-06)
    gain = gain_ref[...].astype(jnp.float32).reshape(1, width)
    normed = (hid[...] * inv_norm * gain).astype(jnp.bfloat16)
    logits = lax.dot_general(
        router_ref[...], normed, (((1,), (1,)), ((), ())), preferred_element_type=jnp.float32
    )
    name = lax.broadcasted_iota(jnp.int32, (experts, tok), 0)
    routes = routes_ref[...]
    routed = name == routes[0:1, :]
    for k in range(1, routes.shape[0]):
        routed = jnp.logical_or(routed, name == routes[k : k + 1, :])
    picked = jnp.where(routed, jnp.exp(logits), 0.0)
    gates = picked / jnp.sum(picked, axis=0, keepdims=True)
    extra = gath.shape[3] - width
    if extra > experts:
        gates = jnp.concatenate([gates, jnp.zeros((extra - experts, tok), jnp.float32)], axis=0)
    gates = jnp.concatenate([gates, jnp.zeros((extra, 128 - tok), jnp.float32)], axis=1)
    gath[0, 0, :, :width] = normed
    gath[0, 0, :, width:] = jnp.transpose(gates)[:tok].astype(jnp.bfloat16)

    sends = []

    def forward(slot):
        first = slot.bit_length()
        for j in range(first, bits):
            there = slot | (1 << j)
            sends.append(
                remote(gath.at[0, slot], gath.at[0, there], gsend.at[there], grecv.at[there], peers[j])
            )
            sends[-1].start()
        sends.append(remote(gath.at[0, slot], gath.at[1, slot], ssend.at[slot], srecv.at[slot], sib))
        sends[-1].start()

    def arrived(slot):
        remote(gath.at[0, slot], gath.at[0, slot], gsend.at[slot], grecv.at[slot], sib).wait_recv()

    def arrived_sib(slot):
        remote(gath.at[0, slot], gath.at[1, slot], ssend.at[slot], srecv.at[slot], sib).wait_recv()

    half = n // 2
    forward(0)
    for slot in range(1, half):
        arrived(slot)
        forward(slot)

    expert = g * n + d
    size = min(8, half)
    rows = 2 * size * tok

    def gate_up(base, t, tile):
        x = gath[:, pl.ds(base, size), :, :width].reshape(rows, width)
        gate = jnp.dot(x, wgu[:, t : t + tile], preferred_element_type=jnp.float32)
        up = jnp.dot(x, wgu[:, ff + t : ff + t + tile], preferred_element_type=jnp.float32)
        act[:, :, :, t : t + tile] = (
            (gate / (1.0 + jnp.exp(-gate)) * up).astype(jnp.bfloat16).reshape(2, size, tok, tile)
        )

    def down(base, start, count):
        span = slice(start, start + count)
        own_rows = 2 * count * tok
        weights = gath[:, base + start : base + start + count, :, width:]
        weights = weights.reshape(own_rows, extra).astype(jnp.float32)
        mine = lax.broadcasted_iota(jnp.int32, (own_rows, extra), 1) == expert
        weight = jnp.sum(jnp.where(mine, weights, 0.0), axis=1, keepdims=True)
        x = act[:, span].reshape(own_rows, ff)
        tile = 512
        for t in range(0, width, tile):
            y = jnp.dot(x, wd[:, t : t + tile], preferred_element_type=jnp.float32)
            y = (y * weight).astype(jnp.bfloat16).reshape(2, count, tok, tile)
            part[:, base + start : base + start + count, :, t : t + tile] = y

    FT = 256
    for slot in range(half):
        arrived_sib(slot)
    load_gu.wait()
    pending = list(range(half, n))
    tiles = list(range(0, ff, FT))
    for at in range(0, half, size):
        for t in tiles:
            gate_up(at, t, FT)
            if at == 0:
                count = -(-half // len(tiles))
                for slot in pending[:count]:
                    arrived(slot)
                    forward(slot)
                pending = pending[count:]
        if at == 0:
            load_d.wait()
        down(at, 0, size)

    def give(slot):
        sends.append(remote(part.at[1, slot], rsib.at[slot], bsend.at[slot], brecv.at[slot], sib))
        sends[-1].start()

    def add_to(slot, more):
        part[0, slot] = (part[0, slot].astype(jnp.float32) + more.astype(jnp.float32)).astype(
            jnp.bfloat16
        )

    def taken(slot):
        remote(part.at[1, slot], rsib.at[slot], bsend.at[slot], brecv.at[slot], sib).wait_recv()
        add_to(slot, rsib[slot])

    order = [bits - 2, bits - 1] + list(range(bits - 3, -1, -1)) if bits >= 2 else [0]
    first_bit = 1 << order[0]

    def ship(slot, step):
        sends.append(
            remote(
                part.at[0, slot],
                racc.at[slot],
                rsend.at[slot],
                rrecv.at[slot],
                peers[order[step]],
            )
        )
        sends[-1].start()

    def received(source):
        remote(part.at[0, 0], racc.at[source], rsend.at[source], rrecv.at[source], sib).wait_recv()

    def absorb(slot, step):
        source = slot | (1 << order[step])
        received(source)
        add_to(slot, racc[source])

    early = [s for s in range(half) if s & first_bit] + [s for s in range(half) if not s & first_bit]
    for slot in early:
        give(slot)
    for slot in range(half, n):
        arrived_sib(slot)
    waiting = list(early)
    for at in range(half, n, size):
        for t in tiles:
            gate_up(at, t, FT)
            if at == half:
                count = -(-half // len(tiles))
                for slot in waiting[:count]:
                    taken(slot)
                    if slot & first_bit:
                        ship(slot, 0)
                waiting = waiting[count:]
        cut = size // 2
        down(at, cut, size - cut)
        for slot in reversed(range(at + cut, at + size)):
            give(slot)
        down(at, 0, cut)
        for slot in reversed(range(at, at + cut)):
            give(slot)
    for slot in reversed(range(half, n)):
        taken(slot)
        if slot & first_bit:
            ship(slot, 0)

    live = [s for s in range(n) if not s & first_bit]
    for step in range(1, len(order)):
        out_going = [s for s in live if s & (1 << order[step])]
        staying = [s for s in live if not s & (1 << order[step])]
        for s in reversed(out_going):
            absorb(s, step - 1)
            ship(s, step)
        for s in reversed(staying):
            absorb(s, step - 1)
        live = staying
    source = 1 << order[-1]
    received(source)
    out_ref[...] = (
        hid[...] + (part[0, 0].astype(jnp.float32) + racc[source].astype(jnp.float32))
    ).astype(jnp.bfloat16)
    for copy in sends:
        copy.wait_send()


def layer(n, lens, queries, latest, cache, wo, residual, gain, router, routes, gate_up, down):
    tok, width = residual.shape
    bits = n.bit_length() - 1
    extra = -(-router.shape[0] // 128) * 128
    size = min(8, n // 2)
    halves, tokens, q_width = queries.shape
    per_half = tokens // ROWS_STEP
    tiles = width // OUT_TILE
    bf16, f32 = jnp.bfloat16, jnp.float32
    dma = pltpu.SemaphoreType.DMA
    vmem = pl.BlockSpec(memory_space=pltpu.VMEM)
    smem = pl.BlockSpec(memory_space=pltpu.SMEM)
    hbm = pl.BlockSpec(memory_space=pl.ANY)
    return pl.pallas_call(
        functools.partial(layer_kernel, n, bits),
        out_shape=jax.ShapeDtypeStruct((tok, width), bf16),
        in_specs=[smem, vmem, vmem, hbm, hbm, vmem, vmem, vmem, vmem, hbm, hbm],
        out_specs=vmem,
        scratch_shapes=[
            pltpu.VMEM((halves, per_half, ROWS_STEP) + cache.shape[2:], bf16),
            pltpu.VMEM(wo.shape, bf16),
            pltpu.VMEM(gate_up.shape[1:], bf16),
            pltpu.VMEM(down.shape[1:], bf16),
            pltpu.VMEM((halves, tokens, q_width // HEAD_SIZE, HEAD_SIZE), f32),
            pltpu.VMEM((halves * per_half, ROWS_STEP, q_width), f32),
            pltpu.VMEM((tiles, halves, tokens, OUT_TILE), f32),
            pltpu.VMEM((tiles, tok, OUT_TILE), f32),
            pltpu.VMEM((tok, width), f32),
            pltpu.VMEM((2, n, tok, width + extra), bf16),
            pltpu.VMEM((2, size, tok, down.shape[1]), bf16),
            pltpu.VMEM((2, n, tok, width), bf16),
            pltpu.VMEM((n, tok, width), bf16),
            pltpu.VMEM((n, tok, width), bf16),
            dma((halves, per_half)),
            dma((3,)),
            dma((tiles,)),
            dma((tiles,)),
        ]
        + [dma((n,))] * 8,
        compiler_params=pltpu.CompilerParams(
            collective_id=0, has_side_effects=True, vmem_limit_bytes=VMEM_LIMIT
        ),
        name="layer",
    )(lens, queries, latest, cache, wo, residual, gain, router, routes, gate_up, down)


def solution(mesh):
    n = mesh.shape["dev"]

    def per_device(
        residual_in,
        queries,
        latest_key_value,
        key_value_cache,
        cache_len,
        out_weight,
        norm_gain,
        router_weight,
        routes,
        expert_gate_up,
        expert_down,
    ):
        return layer(
            n,
            cache_len,
            queries,
            latest_key_value,
            key_value_cache,
            out_weight,
            residual_in,
            norm_gain,
            router_weight.T,
            routes.T,
            expert_gate_up,
            expert_down,
        )

    placed = (
        P(("grp", "dev"), None),
        P(None, "dev", "grp"),
        P(None, "dev", "grp", None),
        P(None, "dev", "grp", None, None),
        P(None, "dev"),
        P("grp", None),
        P(),
        P(),
        P(("grp", "dev"), None),
        P(("grp", "dev"), None, None),
        P(("grp", "dev"), None, None),
    )
    return jax.shard_map(
        per_device, mesh=mesh, in_specs=placed, out_specs=P(("grp", "dev"), None), check_vma=False
    )
```

```python
import functools
import math

import jax
import jax.numpy as jnp
from jax import lax
from jax.experimental import pallas as pl
from jax.experimental.pallas import tpu as pltpu
from jax.sharding import PartitionSpec as P

HEAD_SIZE = 128
MESH = pl.DeviceIdType.MESH
ROWS_STEP = 8
OUT_TILE = 512
VMEM_LIMIT = 60 * 1024 * 1024


def plan(n, bits):
    hops = [3.2 if j == 0 else 2.0 for j in range(bits)]

    def due(slot):
        return sum(hops[j] for j in range(bits) if slot & (1 << j))

    slots = sorted(range(n), key=lambda slot: (due(slot), slot))
    chunks = [n // 4, n // 2, n // 4] if n <= 16 else [8] * (n // 8)
    return slots, chunks


def layer_kernel(
    n,
    bits,
    lens_ref,
    q_ref,
    new_ref,
    cache_hbm,
    wo_hbm,
    res_ref,
    gain_ref,
    router_ref,
    routes_ref,
    wgu_hbm,
    wd_hbm,
    out_ref,
    kv,
    wo,
    wgu,
    wd,
    qs,
    att,
    pout,
    xsib,
    hid,
    gath,
    act,
    part,
    rsib,
    racc,
    ksem,
    wsem,
    xsend,
    xrecv,
    gsend,
    grecv,
    ssend,
    srecv,
    bsend,
    brecv,
    rsend,
    rrecv,
):
    g = lax.axis_index("grp")
    d = lax.axis_index("dev")
    tok, width = res_ref.shape
    experts = router_ref.shape[0]
    ff = wd.shape[0]
    sib = (1 - g, d)
    halves, tokens = q_ref.shape[:2]
    per_half = tokens // ROWS_STEP
    steps = halves * per_half
    kv_heads, positions = cache_hbm.shape[2:4]
    q_heads = q_ref.shape[2] // HEAD_SIZE
    group = q_heads // kv_heads
    scale = 1.0 / math.sqrt(HEAD_SIZE)

    def load_kv(half, s):
        return pltpu.make_async_copy(
            cache_hbm.at[half, pl.ds(s * ROWS_STEP, ROWS_STEP)],
            kv.at[half, s],
            ksem.at[half, s],
        )

    load_o = pltpu.make_async_copy(wo_hbm, wo, wsem.at[0])
    load_gu = pltpu.make_async_copy(wgu_hbm.at[0], wgu, wsem.at[1])
    load_d = pltpu.make_async_copy(wd_hbm.at[0], wd, wsem.at[2])
    for half in range(halves):
        for s in range(per_half):
            load_kv(half, s).start()

    def peer(j):
        m = 1 << (bits - 1 - j)
        if bits >= 2 and j == bits - 2:
            m = 1 + g
        elif bits >= 2 and j == bits - 1:
            m = 2 - g
        return (g, d + m * (1 - 2 * ((d // m) % 2)))

    peers = [peer(j) for j in range(bits)]
    barrier = pltpu.get_barrier_semaphore()
    for target in peers + [sib]:
        pl.semaphore_signal(barrier, inc=1, device_id=target, device_id_type=MESH)

    def remote(src, dst, send, recv, target):
        return pltpu.make_async_remote_copy(
            src_ref=src,
            dst_ref=dst,
            send_sem=send,
            recv_sem=recv,
            device_id=target,
            device_id_type=MESH,
        )

    for half in range(halves):
        q = q_ref[half].astype(jnp.float32)
        q = jnp.stack([q[:, j * HEAD_SIZE : (j + 1) * HEAD_SIZE] for j in range(q_heads)], axis=0)
        qs[half] = jnp.swapaxes(q, 0, 1)

    pairs = [(r, h) for r in range(ROWS_STEP) for h in range(kv_heads)]

    def attend(i, carry):
        half = i // per_half
        s = i % per_half
        load_kv(half, s).wait()

        @pl.when(i == 0)
        def _():
            load_o.start()

        first = pl.multiple_of(s * ROWS_STEP, ROWS_STEP)
        q = qs[half, pl.ds(first, ROWS_STEP)].reshape(ROWS_STEP, kv_heads, group, HEAD_SIZE)
        new = new_ref[half, pl.ds(first, ROWS_STEP)].astype(jnp.float32)[:, :, None, :]
        own = jnp.exp(jnp.sum(q * new[..., :HEAD_SIZE], axis=-1, keepdims=True) * scale)
        qb = q.astype(jnp.bfloat16)
        place = lax.broadcasted_iota(jnp.int32, (group, positions), 1)
        lens = [lens_ref[half, first + r] for r in range(ROWS_STEP)]
        scores = [
            lax.dot_general(
                qb[r, h],
                kv[half, s, r, h, :, :HEAD_SIZE],
                (((1,), (1,)), ((), ())),
                preferred_element_type=jnp.float32,
            )
            for r, h in pairs
        ]
        raised = [
            jnp.where(place < lens[r], jnp.exp(x * scale), 0.0) for (r, h), x in zip(pairs, scores)
        ]
        inverse = [
            1.0 / (jnp.sum(e, axis=1, keepdims=True) + own[r, h]) for (r, h), e in zip(pairs, raised)
        ]
        weights = [(e * v).astype(jnp.bfloat16) for e, v in zip(raised, inverse)]
        mixed = [
            jnp.dot(w, kv[half, s, r, h, :, HEAD_SIZE:], preferred_element_type=jnp.float32)
            for (r, h), w in zip(pairs, weights)
        ]
        mixed = [
            o
            + (own[r, h] * v).astype(jnp.bfloat16).astype(jnp.float32) * new[r, h, :, HEAD_SIZE:]
            for (r, h), o, v in zip(pairs, mixed, inverse)
        ]
        mixed = jnp.stack(
            [
                jnp.concatenate(mixed[r * kv_heads : (r + 1) * kv_heads], axis=0)
                for r in range(ROWS_STEP)
            ],
            axis=0,
        )
        mixed = jnp.swapaxes(mixed, 0, 1)
        att[i] = jnp.concatenate([mixed[j] for j in range(q_heads)], axis=1)
        return carry

    lax.fori_loop(0, steps, attend, 0)
    load_gu.start()
    load_d.start()
    pl.semaphore_wait(barrier, bits + 1)
    load_o.wait()
    attended = att[...].reshape(halves * tokens, q_heads * HEAD_SIZE).astype(jnp.bfloat16)
    swaps = []
    for t in range(width // OUT_TILE):
        cols = slice(t * OUT_TILE, (t + 1) * OUT_TILE)
        y = jnp.dot(attended, wo[:, cols], preferred_element_type=jnp.float32)
        pout[t] = y.reshape(halves, tokens, OUT_TILE)
        swaps.append(remote(pout.at[t, 1 - g], xsib.at[t], xsend.at[t], xrecv.at[t], sib))
        swaps[-1].start()
    squares = jnp.zeros((tok, 1), jnp.float32)
    for t in range(width // OUT_TILE):
        cols = slice(t * OUT_TILE, (t + 1) * OUT_TILE)
        swaps[t].wait()
        h = res_ref[:, cols].astype(jnp.float32) + (pout[t, g] + xsib[t])
        hid[:, cols] = h
        squares = squares + jnp.sum(h * h, axis=-1, keepdims=True)
    inv_norm = lax.rsqrt(squares * (1.0 / width) + 1e-06)
    gain = gain_ref[...].astype(jnp.float32).reshape(1, width)
    normed = (hid[...] * inv_norm * gain).astype(jnp.bfloat16)
    logits = lax.dot_general(
        router_ref[...], normed, (((1,), (1,)), ((), ())), preferred_element_type=jnp.float32
    )
    name = lax.broadcasted_iota(jnp.int32, (experts, tok), 0)
    routes = routes_ref[...]
    routed = name == routes[0:1, :]
    for k in range(1, routes.shape[0]):
        routed = jnp.logical_or(routed, name == routes[k : k + 1, :])
    picked = jnp.where(routed, jnp.exp(logits), 0.0)
    gates = picked / jnp.sum(picked, axis=0, keepdims=True)
    extra = gath.shape[3] - width
    if extra > experts:
        gates = jnp.concatenate([gates, jnp.zeros((extra - experts, tok), jnp.float32)], axis=0)
    gates = jnp.concatenate([gates, jnp.zeros((extra, 128 - tok), jnp.float32)], axis=1)
    gath[0, 0, :, :width] = normed
    gath[0, 0, :, width:] = jnp.transpose(gates)[:tok].astype(jnp.bfloat16)

    sends = []
    slots, chunks = plan(n, bits)
    place_of = {slot: at for at, slot in enumerate(slots)}
    order = [bits - 2, bits - 1] + list(range(bits - 3, -1, -1))

    def forward(slot):
        at = place_of[slot]
        for j in range(slot.bit_length(), bits):
            there = slot | (1 << j)
            sends.append(
                remote(
                    gath.at[0, at],
                    gath.at[0, place_of[there]],
                    gsend.at[there],
                    grecv.at[there],
                    peers[j],
                )
            )
            sends[-1].start()
        sends.append(remote(gath.at[0, at], gath.at[1, at], ssend.at[slot], srecv.at[slot], sib))
        sends[-1].start()

    def arrived(slot):
        at = gath.at[0, place_of[slot]]
        remote(at, at, gsend.at[slot], grecv.at[slot], sib).wait_recv()

    def arrived_sib(slot):
        at = place_of[slot]
        remote(gath.at[0, at], gath.at[1, at], ssend.at[slot], srecv.at[slot], sib).wait_recv()

    forward(0)
    expert = g * n + d
    FT = 256
    DT = 512

    def gate_up(start, count, t):
        x = gath[:, start : start + count, :, :width].reshape(2 * count * tok, width)
        gate = jnp.dot(x, wgu[:, t : t + FT], preferred_element_type=jnp.float32)
        up = jnp.dot(x, wgu[:, ff + t : ff + t + FT], preferred_element_type=jnp.float32)
        y = (gate / (1.0 + jnp.exp(-gate)) * up).astype(jnp.bfloat16)
        act[:, :count, :, t : t + FT] = y.reshape(2, count, tok, FT)

    def weigh(start, count):
        weights = gath[:, start : start + count, :, width:]
        weights = weights.reshape(2 * count * tok, extra).astype(jnp.float32)
        mine = lax.broadcasted_iota(jnp.int32, weights.shape, 1) == expert
        return jnp.sum(jnp.where(mine, weights, 0.0), axis=1, keepdims=True)

    def down(start, count, t, weight):
        x = act[:, :count].reshape(2 * count * tok, ff)
        y = jnp.dot(x, wd[:, t : t + DT], preferred_element_type=jnp.float32)
        y = (y * weight).astype(jnp.bfloat16).reshape(2, count, tok, DT)
        part[:, start : start + count, :, t : t + DT] = y

    def give(slot):
        at = place_of[slot]
        sends.append(remote(part.at[1, at], rsib.at[slot], bsend.at[slot], brecv.at[slot], sib))
        sends[-1].start()

    def add_to(slot, more):
        at = place_of[slot]
        part[0, at] = (part[0, at].astype(jnp.float32) + more.astype(jnp.float32)).astype(
            jnp.bfloat16
        )

    def ship(slot, step):
        sends.append(
            remote(
                part.at[0, place_of[slot]],
                racc.at[slot],
                rsend.at[slot],
                rrecv.at[slot],
                peers[order[step]],
            )
        )
        sends[-1].start()

    def received(source):
        remote(part.at[0, 0], racc.at[source], rsend.at[source], rrecv.at[source], sib).wait_recv()

    def taken(slot):
        remote(part.at[1, 0], rsib.at[slot], bsend.at[slot], brecv.at[slot], sib).wait_recv()
        add_to(slot, rsib[slot])
        if slot & (1 << order[0]):
            ship(slot, 0)

    def step_of(slot):
        return min(t for t in range(bits) if slot & (1 << order[t]))

    def pump(slot):
        arrived(slot)
        forward(slot)

    def spread(work, points):
        share = -(-len(work) // points)
        return [work[k * share : (k + 1) * share] for k in range(points)]

    points = ff // FT + width // DT
    start = 0
    previous = []
    for c, count in enumerate(chunks):
        now = slots[start : start + count]
        if c == 0:
            for slot in now[1:]:
                pump(slot)
        for slot in now:
            arrived_sib(slot)
        if c == 0:
            load_gu.wait()
        ahead = slots[start + count : start + count + chunks[c + 1]] if c + 1 < len(chunks) else []
        pumps = spread(ahead, points - 1) + [[]]
        takes = spread(sorted(previous, key=lambda s: not s & (1 << order[0])), points - 1) + [[]]
        k = 0
        for t in range(0, ff, FT):
            gate_up(start, count, t)
            for slot in pumps[k]:
                pump(slot)
            for slot in takes[k]:
                taken(slot)
            k += 1
        if c == 0:
            load_d.wait()
        weight = weigh(start, count)
        for t in range(0, width, DT):
            down(start, count, t, weight)
            for slot in pumps[k]:
                pump(slot)
            for slot in takes[k]:
                taken(slot)
            k += 1
        previous = sorted(now, key=lambda s: not s & (1 << order[0]))
        for slot in previous:
            give(slot)
        start += count
    for slot in previous:
        taken(slot)

    for step in range(1, bits):
        for slot in slots[1:]:
            if step_of(slot) == step:
                for t in range(step):
                    source = slot | (1 << order[t])
                    received(source)
                    add_to(slot, racc[source])
                ship(slot, step)
    total = hid[...] + part[0, 0].astype(jnp.float32)
    for t in range(bits):
        received(1 << order[t])
        total = total + racc[1 << order[t]].astype(jnp.float32)
    out_ref[...] = total
    for copy in sends:
        copy.wait_send()


def layer(n, lens, queries, latest, cache, wo, residual, gain, router, routes, gate_up, down):
    tok, width = residual.shape
    bits = n.bit_length() - 1
    extra = -(-router.shape[0] // 128) * 128
    size = max(plan(n, bits)[1])
    halves, tokens, q_width = queries.shape
    per_half = tokens // ROWS_STEP
    tiles = width // OUT_TILE
    bf16, f32 = jnp.bfloat16, jnp.float32
    dma = pltpu.SemaphoreType.DMA
    vmem = pl.BlockSpec(memory_space=pltpu.VMEM)
    smem = pl.BlockSpec(memory_space=pltpu.SMEM)
    hbm = pl.BlockSpec(memory_space=pl.ANY)
    return pl.pallas_call(
        functools.partial(layer_kernel, n, bits),
        out_shape=jax.ShapeDtypeStruct((tok, width), f32),
        in_specs=[smem, vmem, vmem, hbm, hbm, vmem, vmem, vmem, vmem, hbm, hbm],
        out_specs=vmem,
        scratch_shapes=[
            pltpu.VMEM((halves, per_half, ROWS_STEP) + cache.shape[2:], bf16),
            pltpu.VMEM(wo.shape, bf16),
            pltpu.VMEM(gate_up.shape[1:], bf16),
            pltpu.VMEM(down.shape[1:], bf16),
            pltpu.VMEM((halves, tokens, q_width // HEAD_SIZE, HEAD_SIZE), f32),
            pltpu.VMEM((halves * per_half, ROWS_STEP, q_width), f32),
            pltpu.VMEM((tiles, halves, tokens, OUT_TILE), f32),
            pltpu.VMEM((tiles, tok, OUT_TILE), f32),
            pltpu.VMEM((tok, width), f32),
            pltpu.VMEM((2, n, tok, width + extra), bf16),
            pltpu.VMEM((2, size, tok, down.shape[1]), bf16),
            pltpu.VMEM((2, n, tok, width), bf16),
            pltpu.VMEM((n, tok, width), bf16),
            pltpu.VMEM((n, tok, width), bf16),
            dma((halves, per_half)),
            dma((3,)),
            dma((tiles,)),
            dma((tiles,)),
        ]
        + [dma((n,))] * 8,
        compiler_params=pltpu.CompilerParams(
            collective_id=0, has_side_effects=True, vmem_limit_bytes=VMEM_LIMIT
        ),
        name="layer",
    )(lens, queries, latest, cache, wo, residual, gain, router, routes, gate_up, down)


def solution(mesh):
    n = mesh.shape["dev"]

    def per_device(
        residual_in,
        queries,
        latest_key_value,
        key_value_cache,
        cache_len,
        out_weight,
        norm_gain,
        router_weight,
        routes,
        expert_gate_up,
        expert_down,
    ):
        return layer(
            n,
            cache_len,
            queries,
            latest_key_value,
            key_value_cache,
            out_weight,
            residual_in,
            norm_gain,
            router_weight.T,
            routes.T,
            expert_gate_up,
            expert_down,
        ).astype(jnp.bfloat16)

    placed = (
        P(("grp", "dev"), None),
        P(None, "dev", "grp"),
        P(None, "dev", "grp", None),
        P(None, "dev", "grp", None, None),
        P(None, "dev"),
        P("grp", None),
        P(),
        P(),
        P(("grp", "dev"), None),
        P(("grp", "dev"), None, None),
        P(("grp", "dev"), None, None),
    )
    return jax.shard_map(
        per_device, mesh=mesh, in_specs=placed, out_specs=P(("grp", "dev"), None), check_vma=False
    )
```

```python
import functools
import math

import jax
import jax.numpy as jnp
from jax import lax
from jax.experimental import pallas as pl
from jax.experimental.pallas import tpu as pltpu
from jax.sharding import PartitionSpec as P

HEAD_SIZE = 128
MESH = pl.DeviceIdType.MESH
ROWS_STEP = 8
OUT_TILE = 512
FF_TILE = 256
VMEM_LIMIT = 60 * 1024 * 1024


def layer_kernel(
    n,
    bits,
    lens_ref,
    q_ref,
    new_ref,
    cache_hbm,
    wo_hbm,
    res_ref,
    gain_ref,
    router_ref,
    routes_ref,
    wgu_hbm,
    wd_hbm,
    out_ref,
    kv,
    wo,
    wgu,
    wd,
    qs,
    att,
    pout,
    xsib,
    hid,
    gath,
    act,
    part,
    rsib,
    racc,
    ksem,
    wsem,
    xsend,
    xrecv,
    gsend,
    grecv,
    ssend,
    srecv,
    bsend,
    brecv,
    rsend,
    rrecv,
):
    g = lax.axis_index("grp")
    d = lax.axis_index("dev")
    tok, width = res_ref.shape
    experts = router_ref.shape[0]
    ff = wd.shape[0]
    sib = (1 - g, d)
    halves, tokens = q_ref.shape[:2]
    per_half = tokens // ROWS_STEP
    steps = halves * per_half
    kv_heads, positions = cache_hbm.shape[2:4]
    q_heads = q_ref.shape[2] // HEAD_SIZE
    group = q_heads // kv_heads
    scale = 1.0 / math.sqrt(HEAD_SIZE)

    def load_kv(half, s):
        return pltpu.make_async_copy(
            cache_hbm.at[half, pl.ds(s * ROWS_STEP, ROWS_STEP)],
            kv.at[half, s],
            ksem.at[half, s],
        )

    load_o = pltpu.make_async_copy(wo_hbm, wo, wsem.at[0])
    load_gu = pltpu.make_async_copy(wgu_hbm.at[0], wgu, wsem.at[1])
    load_d = pltpu.make_async_copy(wd_hbm.at[0], wd, wsem.at[2])
    for half in range(halves):
        for s in range(per_half):
            load_kv(half, s).start()

    def peer(j):
        m = 1 << (bits - 1 - j)
        if bits >= 2 and j == bits - 2:
            m = 1 + g
        elif bits >= 2 and j == bits - 1:
            m = 2 - g
        return (g, d + m * (1 - 2 * ((d // m) % 2)))

    peers = [peer(j) for j in range(bits)]
    barrier = pltpu.get_barrier_semaphore()
    for target in peers + [sib]:
        pl.semaphore_signal(barrier, inc=1, device_id=target, device_id_type=MESH)

    def remote(src, dst, send, recv, target):
        return pltpu.make_async_remote_copy(
            src_ref=src,
            dst_ref=dst,
            send_sem=send,
            recv_sem=recv,
            device_id=target,
            device_id_type=MESH,
        )

    for half in range(halves):
        q = q_ref[half].astype(jnp.float32)
        q = jnp.stack([q[:, j * HEAD_SIZE : (j + 1) * HEAD_SIZE] for j in range(q_heads)], axis=0)
        qs[half] = jnp.swapaxes(q, 0, 1)

    pairs = [(r, h) for r in range(ROWS_STEP) for h in range(kv_heads)]

    def attend(i, carry):
        half = i // per_half
        s = i % per_half
        load_kv(half, s).wait()

        @pl.when(i == 0)
        def _():
            load_o.start()

        first = pl.multiple_of(s * ROWS_STEP, ROWS_STEP)
        q = qs[half, pl.ds(first, ROWS_STEP)].reshape(ROWS_STEP, kv_heads, group, HEAD_SIZE)
        new = new_ref[half, pl.ds(first, ROWS_STEP)].astype(jnp.float32)[:, :, None, :]
        own = jnp.exp(jnp.sum(q * new[..., :HEAD_SIZE], axis=-1, keepdims=True) * scale)
        qb = q.astype(jnp.bfloat16)
        place = lax.broadcasted_iota(jnp.int32, (group, positions), 1)
        lens = [lens_ref[half, first + r] for r in range(ROWS_STEP)]
        scores = [
            lax.dot_general(
                qb[r, h],
                kv[half, s, r, h, :, :HEAD_SIZE],
                (((1,), (1,)), ((), ())),
                preferred_element_type=jnp.float32,
            )
            for r, h in pairs
        ]
        raised = [
            jnp.where(place < lens[r], jnp.exp(x * scale), 0.0) for (r, h), x in zip(pairs, scores)
        ]
        inverse = [
            1.0 / (jnp.sum(e, axis=1, keepdims=True) + own[r, h]) for (r, h), e in zip(pairs, raised)
        ]
        weights = [(e * v).astype(jnp.bfloat16) for e, v in zip(raised, inverse)]
        mixed = [
            jnp.dot(w, kv[half, s, r, h, :, HEAD_SIZE:], preferred_element_type=jnp.float32)
            for (r, h), w in zip(pairs, weights)
        ]
        mixed = [
            o
            + (own[r, h] * v).astype(jnp.bfloat16).astype(jnp.float32) * new[r, h, :, HEAD_SIZE:]
            for (r, h), o, v in zip(pairs, mixed, inverse)
        ]
        mixed = jnp.stack(
            [
                jnp.concatenate(mixed[r * kv_heads : (r + 1) * kv_heads], axis=0)
                for r in range(ROWS_STEP)
            ],
            axis=0,
        )
        mixed = jnp.swapaxes(mixed, 0, 1)
        att[i] = jnp.concatenate([mixed[j] for j in range(q_heads)], axis=1)
        return carry

    lax.fori_loop(0, steps, attend, 0)
    load_gu.start()
    load_d.start()
    pl.semaphore_wait(barrier, bits + 1)
    load_o.wait()
    attended = att[...].reshape(halves * tokens, q_heads * HEAD_SIZE).astype(jnp.bfloat16)
    swaps = []
    for t in range(width // OUT_TILE):
        cols = slice(t * OUT_TILE, (t + 1) * OUT_TILE)
        y = jnp.dot(attended, wo[:, cols], preferred_element_type=jnp.float32)
        pout[t] = y.reshape(halves, tokens, OUT_TILE)
        swaps.append(remote(pout.at[t, 1 - g], xsib.at[t], xsend.at[t], xrecv.at[t], sib))
        swaps[-1].start()
    squares = jnp.zeros((tok, 1), jnp.float32)
    for t in range(width // OUT_TILE):
        cols = slice(t * OUT_TILE, (t + 1) * OUT_TILE)
        swaps[t].wait()
        h = res_ref[:, cols].astype(jnp.float32) + (pout[t, g] + xsib[t])
        hid[:, cols] = h
        squares = squares + jnp.sum(h * h, axis=-1, keepdims=True)
    inv_norm = lax.rsqrt(squares * (1.0 / width) + 1e-06)
    gain = gain_ref[...].astype(jnp.float32).reshape(1, width)
    normed = (hid[...] * inv_norm * gain).astype(jnp.bfloat16)
    logits = lax.dot_general(
        router_ref[...], normed, (((1,), (1,)), ((), ())), preferred_element_type=jnp.float32
    )
    name = lax.broadcasted_iota(jnp.int32, (experts, tok), 0)
    routes = routes_ref[...]
    routed = name == routes[0:1, :]
    for k in range(1, routes.shape[0]):
        routed = jnp.logical_or(routed, name == routes[k : k + 1, :])
    picked = jnp.where(routed, jnp.exp(logits), 0.0)
    gates = picked / jnp.sum(picked, axis=0, keepdims=True)
    extra = gath.shape[3] - width
    if extra > experts:
        gates = jnp.concatenate([gates, jnp.zeros((extra - experts, tok), jnp.float32)], axis=0)
    gates = jnp.concatenate([gates, jnp.zeros((extra, 128 - tok), jnp.float32)], axis=1)
    gath[0, 0, :, :width] = normed
    gath[0, 0, :, width:] = jnp.transpose(gates)[:tok].astype(jnp.bfloat16)

    sends = []

    def forward(slot):
        first = slot.bit_length()
        for j in range(first, bits):
            there = slot | (1 << j)
            sends.append(
                remote(gath.at[0, slot], gath.at[0, there], gsend.at[there], grecv.at[there], peers[j])
            )
            sends[-1].start()
        sends.append(remote(gath.at[0, slot], gath.at[1, slot], ssend.at[slot], srecv.at[slot], sib))
        sends[-1].start()

    def arrived(slot):
        remote(gath.at[0, slot], gath.at[0, slot], gsend.at[slot], grecv.at[slot], sib).wait_recv()

    def arrived_sib(slot):
        remote(gath.at[0, slot], gath.at[1, slot], ssend.at[slot], srecv.at[slot], sib).wait_recv()

    half = n // 2
    quarter = n // 4
    expert = g * n + d
    size = min(8, half)
    rows = 2 * size * tok
    tiles = width // OUT_TILE

    def due(slot):
        return sum((3 if j == 0 else 2) for j in range(bits) if slot & (1 << j))

    forward(0)
    for slot in sorted(range(1, half), key=due):
        arrived(slot)
        forward(slot)

    def gate_up(base, t):
        x = gath[:, base : base + size, :, :width].reshape(rows, width)
        gate = jnp.dot(x, wgu[:, t : t + FF_TILE], preferred_element_type=jnp.float32)
        up = jnp.dot(x, wgu[:, ff + t : ff + t + FF_TILE], preferred_element_type=jnp.float32)
        act[:, t : t + FF_TILE] = (gate / (1.0 + jnp.exp(-gate)) * up).astype(jnp.bfloat16)

    def weigh(base):
        weights = gath[:, base : base + size, :, width:].reshape(rows, extra).astype(jnp.float32)
        mine = lax.broadcasted_iota(jnp.int32, (rows, extra), 1) == expert
        return jnp.sum(jnp.where(mine, weights, 0.0), axis=1, keepdims=True)

    def down(base, t, weight):
        y = jnp.dot(
            act[...], wd[:, t * OUT_TILE : (t + 1) * OUT_TILE], preferred_element_type=jnp.float32
        )
        part[t, :, base : base + size] = (
            (y * weight).astype(jnp.bfloat16).reshape(2, size, tok, OUT_TILE)
        )

    def give(t, which):
        span = pl.ds(which * half, half)
        sends.append(
            remote(
                part.at[t, 1, span], rsib.at[t, span], bsend.at[t, which], brecv.at[t, which], sib
            )
        )
        sends[-1].start()

    def add_to(t, low, high, more):
        part[t, 0, low:high] = (
            part[t, 0, low:high].astype(jnp.float32) + more.astype(jnp.float32)
        ).astype(jnp.bfloat16)

    def hop(t, low, count, index, j):
        span = pl.ds(low, count)
        return remote(
            part.at[t, 0, span], racc.at[t, span], rsend.at[t, index], rrecv.at[t, index], peers[j]
        )

    def ship(*where):
        sends.append(hop(*where))
        sends[-1].start()

    def take(t, which):
        span = pl.ds(which * half, half)
        remote(
            part.at[t, 1, span], rsib.at[t, span], bsend.at[t, which], brecv.at[t, which], sib
        ).wait_recv()
        low = which * half
        far = low + quarter
        add_to(t, far, far + quarter, rsib[t, far : far + quarter])
        ship(t, far, quarter, which, bits - 2)
        add_to(t, low, far, rsib[t, low:far])

    def second(t):
        hop(t, half + quarter, quarter, 1, bits - 2).wait_recv()
        add_to(t, half, half + quarter, racc[t, half + quarter : n])
        ship(t, half, quarter, 2, bits - 1)

    def third(t):
        hop(t, quarter, quarter, 0, bits - 2).wait_recv()
        add_to(t, 0, quarter, racc[t, quarter:half])
        hop(t, half, quarter, 2, bits - 1).wait_recv()
        add_to(t, 0, quarter, racc[t, half : half + quarter])
        if bits > 2:
            m = quarter // 2
            ship(t, m, m, 3, bits - 3)

    def later(t, k):
        m = quarter >> (k + 1)
        hop(t, m, m, 3 + k, bits - 3 - k).wait_recv()
        add_to(t, 0, m, racc[t, m : 2 * m])
        ship(t, m // 2, m // 2, 4 + k, bits - 4 - k)

    def last(t):
        cols = slice(t * OUT_TILE, (t + 1) * OUT_TILE)
        total = hid[:, cols] + part[t, 0, 0].astype(jnp.float32)
        if bits > 2:
            hop(t, 1, 1, bits, 0).wait_recv()
            total = total + racc[t, 1].astype(jnp.float32)
        out_ref[:, cols] = total.astype(jnp.bfloat16)

    for slot in range(half):
        arrived_sib(slot)
    load_gu.wait()
    pending = sorted(range(half, n), key=due)
    share = -(-half // 4)
    for at in range(0, half, size):
        for t in range(0, ff, FF_TILE):
            gate_up(at, t)
            if at == 0:
                for slot in pending[:share]:
                    arrived(slot)
                    forward(slot)
                pending = pending[share:]
        if at == 0:
            load_d.wait()
        weight = weigh(at)
        for t in range(tiles):
            down(at, t, weight)
            if at + size == half:
                give(t, 0)
            if at == 0:
                for slot in pending[:share]:
                    arrived(slot)
                    forward(slot)
                pending = pending[share:]
    for slot in pending:
        arrived(slot)
        forward(slot)
    for slot in range(half, n):
        arrived_sib(slot)
    waiting = list(range(tiles))
    for at in range(half, n, size):
        for t in range(0, ff, FF_TILE):
            gate_up(at, t)
            for k in waiting[:2]:
                take(k, 0)
            waiting = waiting[2:]
        weight = weigh(at)
        for t in range(tiles):
            down(at, t, weight)
            if at + size == n:
                give(t, 1)
                if t >= 2:
                    take(t - 2, 1)
    for k in waiting:
        take(k, 0)
    stages = [second, third] + [functools.partial(later, k=k) for k in range(bits - 3)] + [last]
    for t in range(tiles - 2, tiles):
        take(t, 1)
        second(t - 2)
    for turn in range(1, tiles + len(stages)):
        for k in range(len(stages)):
            t = turn - k
            if 0 <= t < tiles and not (k == 0 and t < 2):
                stages[k](t)
    for copy in sends:
        copy.wait_send()


def layer(n, lens, queries, latest, cache, wo, residual, gain, router, routes, gate_up, down):
    tok, width = residual.shape
    bits = n.bit_length() - 1
    extra = -(-router.shape[0] // 128) * 128
    size = min(8, n // 2)
    halves, tokens, q_width = queries.shape
    per_half = tokens // ROWS_STEP
    tiles = width // OUT_TILE
    bf16, f32 = jnp.bfloat16, jnp.float32
    dma = pltpu.SemaphoreType.DMA
    vmem = pl.BlockSpec(memory_space=pltpu.VMEM)
    smem = pl.BlockSpec(memory_space=pltpu.SMEM)
    hbm = pl.BlockSpec(memory_space=pl.ANY)
    return pl.pallas_call(
        functools.partial(layer_kernel, n, bits),
        out_shape=jax.ShapeDtypeStruct((tok, width), bf16),
        in_specs=[smem, vmem, vmem, hbm, hbm, vmem, vmem, vmem, vmem, hbm, hbm],
        out_specs=vmem,
        scratch_shapes=[
            pltpu.VMEM((halves, per_half, ROWS_STEP) + cache.shape[2:], bf16),
            pltpu.VMEM(wo.shape, bf16),
            pltpu.VMEM(gate_up.shape[1:], bf16),
            pltpu.VMEM(down.shape[1:], bf16),
            pltpu.VMEM((halves, tokens, q_width // HEAD_SIZE, HEAD_SIZE), f32),
            pltpu.VMEM((halves * per_half, ROWS_STEP, q_width), f32),
            pltpu.VMEM((tiles, halves, tokens, OUT_TILE), f32),
            pltpu.VMEM((tiles, tok, OUT_TILE), f32),
            pltpu.VMEM((tok, width), f32),
            pltpu.VMEM((2, n, tok, width + extra), bf16),
            pltpu.VMEM((2 * size * tok, down.shape[1]), bf16),
            pltpu.VMEM((tiles, 2, n, tok, OUT_TILE), bf16),
            pltpu.VMEM((tiles, n, tok, OUT_TILE), bf16),
            pltpu.VMEM((tiles, n, tok, OUT_TILE), bf16),
            dma((halves, per_half)),
            dma((3,)),
            dma((tiles,)),
            dma((tiles,)),
            dma((n,)),
            dma((n,)),
            dma((n,)),
            dma((n,)),
            dma((tiles, 2)),
            dma((tiles, 2)),
            dma((tiles, bits + 1)),
            dma((tiles, bits + 1)),
        ],
        compiler_params=pltpu.CompilerParams(
            collective_id=0, has_side_effects=True, vmem_limit_bytes=VMEM_LIMIT
        ),
        name="layer",
    )(lens, queries, latest, cache, wo, residual, gain, router, routes, gate_up, down)


def solution(mesh):
    n = mesh.shape["dev"]

    def per_device(
        residual_in,
        queries,
        latest_key_value,
        key_value_cache,
        cache_len,
        out_weight,
        norm_gain,
        router_weight,
        routes,
        expert_gate_up,
        expert_down,
    ):
        return layer(
            n,
            cache_len,
            queries,
            latest_key_value,
            key_value_cache,
            out_weight,
            residual_in,
            norm_gain,
            router_weight.T,
            routes.T,
            expert_gate_up,
            expert_down,
        )

    placed = (
        P(("grp", "dev"), None),
        P(None, "dev", "grp"),
        P(None, "dev", "grp", None),
        P(None, "dev", "grp", None, None),
        P(None, "dev"),
        P("grp", None),
        P(),
        P(),
        P(("grp", "dev"), None),
        P(("grp", "dev"), None, None),
        P(("grp", "dev"), None, None),
    )
    return jax.shard_map(
        per_device, mesh=mesh, in_specs=placed, out_specs=P(("grp", "dev"), None), check_vma=False
    )
```

```python
import functools
import math

import jax
import jax.numpy as jnp
from jax import lax
from jax.experimental import pallas as pl
from jax.experimental.pallas import tpu as pltpu
from jax.sharding import PartitionSpec as P

HEAD_SIZE = 128
MESH = pl.DeviceIdType.MESH
ROWS_STEP = 8
OUT_TILE = 512
VMEM_LIMIT = 60 * 1024 * 1024


def layer_kernel(
    n,
    bits,
    lens_ref,
    q_ref,
    new_ref,
    cache_hbm,
    wo_hbm,
    res_ref,
    gain_ref,
    router_ref,
    routes_ref,
    wgu_hbm,
    wd_hbm,
    out_ref,
    kv,
    wo,
    wgu,
    wd,
    qs,
    att,
    pout,
    xsib,
    hid,
    gath,
    act,
    part,
    rsib,
    racc,
    ksem,
    wsem,
    xsend,
    xrecv,
    gsend,
    grecv,
    ssend,
    srecv,
    bsend,
    brecv,
    rsend,
    rrecv,
):
    g = lax.axis_index("grp")
    d = lax.axis_index("dev")
    tok, width = res_ref.shape
    experts = router_ref.shape[0]
    ff = wd.shape[0]
    sib = (1 - g, d)
    halves, tokens = q_ref.shape[:2]
    per_half = tokens // ROWS_STEP
    steps = halves * per_half
    kv_heads, positions = cache_hbm.shape[2:4]
    q_heads = q_ref.shape[2] // HEAD_SIZE
    group = q_heads // kv_heads
    scale = 1.0 / math.sqrt(HEAD_SIZE)

    def load_kv(half, s):
        return pltpu.make_async_copy(
            cache_hbm.at[half, pl.ds(s * ROWS_STEP, ROWS_STEP)],
            kv.at[half, s],
            ksem.at[half, s],
        )

    load_o = pltpu.make_async_copy(wo_hbm, wo, wsem.at[0])
    load_gu = pltpu.make_async_copy(wgu_hbm.at[0], wgu, wsem.at[1])
    load_d = pltpu.make_async_copy(wd_hbm.at[0], wd, wsem.at[2])
    for half in range(halves):
        for s in range(per_half):
            load_kv(half, s).start()

    def peer(j):
        m = 1 << (bits - 1 - j)
        if bits >= 2 and j == bits - 2:
            m = 1 + g
        elif bits >= 2 and j == bits - 1:
            m = 2 - g
        return (g, d + m * (1 - 2 * ((d // m) % 2)))

    peers = [peer(j) for j in range(bits)]
    barrier = pltpu.get_barrier_semaphore()
    for target in peers + [sib]:
        pl.semaphore_signal(barrier, inc=1, device_id=target, device_id_type=MESH)

    def remote(src, dst, send, recv, target):
        return pltpu.make_async_remote_copy(
            src_ref=src,
            dst_ref=dst,
            send_sem=send,
            recv_sem=recv,
            device_id=target,
            device_id_type=MESH,
        )

    for half in range(halves):
        q = q_ref[half].astype(jnp.float32)
        q = jnp.stack([q[:, j * HEAD_SIZE : (j + 1) * HEAD_SIZE] for j in range(q_heads)], axis=0)
        qs[half] = jnp.swapaxes(q, 0, 1)

    pairs = [(r, h) for r in range(ROWS_STEP) for h in range(kv_heads)]

    def attend(i, carry):
        half = i // per_half
        s = i % per_half
        load_kv(half, s).wait()

        @pl.when(i == 0)
        def _():
            load_o.start()

        first = pl.multiple_of(s * ROWS_STEP, ROWS_STEP)
        q = qs[half, pl.ds(first, ROWS_STEP)].reshape(ROWS_STEP, kv_heads, group, HEAD_SIZE)
        new = new_ref[half, pl.ds(first, ROWS_STEP)].astype(jnp.float32)[:, :, None, :]
        own = jnp.exp(jnp.sum(q * new[..., :HEAD_SIZE], axis=-1, keepdims=True) * scale)
        qb = q.astype(jnp.bfloat16)
        place = lax.broadcasted_iota(jnp.int32, (group, positions), 1)
        lens = [lens_ref[half, first + r] for r in range(ROWS_STEP)]
        scores = [
            lax.dot_general(
                qb[r, h],
                kv[half, s, r, h, :, :HEAD_SIZE],
                (((1,), (1,)), ((), ())),
                preferred_element_type=jnp.float32,
            )
            for r, h in pairs
        ]
        raised = [
            jnp.where(place < lens[r], jnp.exp(x * scale), 0.0) for (r, h), x in zip(pairs, scores)
        ]
        inverse = [
            1.0 / (jnp.sum(e, axis=1, keepdims=True) + own[r, h]) for (r, h), e in zip(pairs, raised)
        ]
        weights = [(e * v).astype(jnp.bfloat16) for e, v in zip(raised, inverse)]
        mixed = [
            jnp.dot(w, kv[half, s, r, h, :, HEAD_SIZE:], preferred_element_type=jnp.float32)
            for (r, h), w in zip(pairs, weights)
        ]
        mixed = [
            o
            + (own[r, h] * v).astype(jnp.bfloat16).astype(jnp.float32) * new[r, h, :, HEAD_SIZE:]
            for (r, h), o, v in zip(pairs, mixed, inverse)
        ]
        mixed = jnp.stack(
            [
                jnp.concatenate(mixed[r * kv_heads : (r + 1) * kv_heads], axis=0)
                for r in range(ROWS_STEP)
            ],
            axis=0,
        )
        mixed = jnp.swapaxes(mixed, 0, 1)
        att[i] = jnp.concatenate([mixed[j] for j in range(q_heads)], axis=1)
        return carry

    lax.fori_loop(0, steps, attend, 0)
    load_gu.start()
    load_d.start()
    pl.semaphore_wait(barrier, bits + 1)
    load_o.wait()
    attended = att[...].reshape(halves * tokens, q_heads * HEAD_SIZE).astype(jnp.bfloat16)
    sends = []
    parts = len(gath)

    def forward(c, slot):
        for j in range(slot.bit_length(), bits):
            there = slot | (1 << j)
            sends.append(
                remote(
                    gath[c].at[0, slot],
                    gath[c].at[0, there],
                    gsend.at[c, there],
                    grecv.at[c, there],
                    peers[j],
                )
            )
            sends[-1].start()
        sends.append(
            remote(
                gath[c].at[0, slot],
                gath[c].at[1, slot],
                ssend.at[c, slot],
                srecv.at[c, slot],
                sib,
            )
        )
        sends[-1].start()

    def pump(c, slot):
        at = gath[c].at[0, slot]
        remote(at, at, gsend.at[c, slot], grecv.at[c, slot], sib).wait_recv()
        forward(c, slot)

    def arrived_sib(slot):
        for c in range(parts):
            remote(
                gath[c].at[0, slot],
                gath[c].at[1, slot],
                ssend.at[c, slot],
                srecv.at[c, slot],
                sib,
            ).wait_recv()

    tiles = width // OUT_TILE
    per_part = tiles // parts
    wide = width // parts
    extra = gath[-1].shape[3] - wide
    swaps = []

    def project(t):
        y = jnp.dot(
            attended, wo[:, t * OUT_TILE : (t + 1) * OUT_TILE], preferred_element_type=jnp.float32
        )
        pout[t] = y.reshape(halves, tokens, OUT_TILE)
        swaps.append(remote(pout.at[t, 1 - g], xsib.at[t], xsend.at[t], xrecv.at[t], sib))
        swaps[-1].start()

    def settle(c):
        squares = jnp.zeros((tok, 1), jnp.float32)
        for t in range(c * per_part, (c + 1) * per_part):
            cols = slice(t * OUT_TILE, (t + 1) * OUT_TILE)
            swaps[t].wait()
            h = res_ref[:, cols].astype(jnp.float32) + (pout[t, g] + xsib[t])
            hid[:, cols] = h
            squares = squares + jnp.sum(h * h, axis=-1, keepdims=True)
        cols = slice(c * wide, (c + 1) * wide)
        gain = gain_ref[...].astype(jnp.float32).reshape(1, width)[:, cols]
        scaled = (hid[:, cols] * gain).astype(jnp.bfloat16)
        gath[c][0, 0, :, :wide] = scaled
        return squares, scaled

    def partial_logits(c, scaled):
        return lax.dot_general(
            router_ref[:, c * wide : (c + 1) * wide],
            scaled,
            (((1,), (1,)), ((), ())),
            preferred_element_type=jnp.float32,
        )

    for t in range(per_part + 1):
        project(t)
    squares, scaled = settle(0)
    forward(0, 0)
    logits = partial_logits(0, scaled)
    for t in range(per_part + 1, tiles):
        project(t)
    more, scaled = settle(1)
    logits = logits + partial_logits(1, scaled)
    inv_norm = lax.rsqrt((squares + more) * (1.0 / width) + 1e-06)
    square = jnp.broadcast_to(inv_norm, (tok, 128))
    square = jnp.concatenate([square, jnp.zeros((128 - tok, 128), jnp.float32)], axis=0)
    inv_row = jnp.transpose(square)[0:1, :tok]
    logits = logits * inv_row
    name = lax.broadcasted_iota(jnp.int32, (experts, tok), 0)
    routes = routes_ref[...]
    routed = name == routes[0:1, :]
    for k in range(1, routes.shape[0]):
        routed = jnp.logical_or(routed, name == routes[k : k + 1, :])
    picked = jnp.where(routed, jnp.exp(logits), 0.0)
    gates = picked / jnp.sum(picked, axis=0, keepdims=True)
    if extra > experts:
        gates = jnp.concatenate([gates, jnp.zeros((extra - experts, tok), jnp.float32)], axis=0)
    gates = jnp.concatenate([gates, jnp.zeros((extra, 128 - tok), jnp.float32)], axis=1)
    gates = jnp.transpose(gates)[:tok]
    lane = lax.broadcasted_iota(jnp.int32, (tok, extra), 1)
    high = inv_norm.astype(jnp.bfloat16).astype(jnp.float32)
    gates = jnp.where(lane == extra - 2, high, gates)
    gates = jnp.where(lane == extra - 1, inv_norm - high, gates)
    gath[1][0, 0, :, wide:] = gates.astype(jnp.bfloat16)
    forward(1, 0)

    half = n // 2
    early = list(range(1, half))
    lead = min(3, len(early))
    for slot in early[:lead]:
        pump(0, slot)
    for k, slot in enumerate(early):
        if k + lead < len(early):
            pump(0, early[k + lead])
        pump(1, slot)

    expert = g * n + d
    size = min(8, half)
    rows = 2 * size * tok

    def notes(base, start, count):
        own = gath[1][:, base + start : base + start + count, :, wide:]
        own = own.reshape(2 * count * tok, extra).astype(jnp.float32)
        return own, lax.broadcasted_iota(jnp.int32, own.shape, 1)

    def gate_up(base, t, tile):
        own, lane = notes(base, 0, size)
        norm = jnp.sum(jnp.where(lane >= extra - 2, own, 0.0), axis=1, keepdims=True)
        x = jnp.concatenate(
            [
                gath[c][:, base : base + size, :, :wide].reshape(rows, wide)
                for c in range(parts)
            ],
            axis=1,
        )
        gate = norm * jnp.dot(x, wgu[:, t : t + tile], preferred_element_type=jnp.float32)
        up = norm * jnp.dot(x, wgu[:, ff + t : ff + t + tile], preferred_element_type=jnp.float32)
        act[:, :, :, t : t + tile] = (
            (gate / (1.0 + jnp.exp(-gate)) * up).astype(jnp.bfloat16).reshape(2, size, tok, tile)
        )

    def down(base, start, count):
        own, lane = notes(base, start, count)
        weight = jnp.sum(jnp.where(lane == expert, own, 0.0), axis=1, keepdims=True)
        x = act[:, start : start + count].reshape(2 * count * tok, ff)
        tile = 512
        for t in range(0, width, tile):
            y = jnp.dot(x, wd[:, t : t + tile], preferred_element_type=jnp.float32)
            y = (y * weight).astype(jnp.bfloat16).reshape(2, count, tok, tile)
            part[:, base + start : base + start + count, :, t : t + tile] = y

    FT = 256
    for slot in range(half):
        arrived_sib(slot)
    load_gu.wait()
    quarter = half // 2
    pending = []
    for low in (half, half + quarter):
        for c in range(parts):
            pending += [(c, slot) for slot in range(low, low + quarter)]
    tiles = list(range(0, ff, FT))
    share = -(-len(pending) // len(tiles))
    for at in range(0, half, size):
        for t in tiles:
            gate_up(at, t, FT)
            if at == 0:
                for c, slot in pending[:share]:
                    pump(c, slot)
                pending = pending[share:]
        if at == 0:
            load_d.wait()
        down(at, 0, size)

    def give(slot):
        sends.append(remote(part.at[1, slot], rsib.at[slot], bsend.at[slot], brecv.at[slot], sib))
        sends[-1].start()

    def add_to(slot, more):
        part[0, slot] = (part[0, slot].astype(jnp.float32) + more.astype(jnp.float32)).astype(
            jnp.bfloat16
        )

    def taken(slot):
        remote(part.at[1, slot], rsib.at[slot], bsend.at[slot], brecv.at[slot], sib).wait_recv()
        add_to(slot, rsib[slot])

    order = [bits - 2, bits - 1] + list(range(bits - 3, -1, -1)) if bits >= 2 else [0]
    first_bit = 1 << order[0]

    def ship(slot, step):
        sends.append(
            remote(
                part.at[0, slot],
                racc.at[slot],
                rsend.at[slot],
                rrecv.at[slot],
                peers[order[step]],
            )
        )
        sends[-1].start()

    def received(source):
        remote(part.at[0, 0], racc.at[source], rsend.at[source], rrecv.at[source], sib).wait_recv()

    def absorb(slot, step):
        source = slot | (1 << order[step])
        received(source)
        add_to(slot, racc[source])

    early = [s for s in range(half) if s & first_bit] + [s for s in range(half) if not s & first_bit]
    for slot in early:
        give(slot)
    for slot in range(half, n):
        arrived_sib(slot)
    waiting = list(early)
    for at in range(half, n, size):
        for t in tiles:
            gate_up(at, t, FT)
            if at == half:
                count = -(-half // len(tiles))
                for slot in waiting[:count]:
                    taken(slot)
                    if slot & first_bit:
                        ship(slot, 0)
                waiting = waiting[count:]
        cut = size // 2
        down(at, cut, size - cut)
        for slot in reversed(range(at + cut, at + size)):
            give(slot)
        down(at, 0, cut)
        for slot in reversed(range(at, at + cut)):
            give(slot)
    for slot in reversed(range(half, n)):
        taken(slot)
        if slot & first_bit:
            ship(slot, 0)

    live = [s for s in range(n) if not s & first_bit]
    for step in range(1, len(order)):
        out_going = [s for s in live if s & (1 << order[step])]
        staying = [s for s in live if not s & (1 << order[step])]
        for s in reversed(out_going):
            absorb(s, step - 1)
            ship(s, step)
        for s in reversed(staying):
            absorb(s, step - 1)
        live = staying
    source = 1 << order[-1]
    received(source)
    out_ref[...] = (
        hid[...] + (part[0, 0].astype(jnp.float32) + racc[source].astype(jnp.float32))
    ).astype(jnp.bfloat16)
    for copy in sends:
        copy.wait_send()


def layer(n, lens, queries, latest, cache, wo, residual, gain, router, routes, gate_up, down):
    tok, width = residual.shape
    bits = n.bit_length() - 1
    extra = -(-(router.shape[0] + 2) // 128) * 128
    size = min(8, n // 2)
    halves, tokens, q_width = queries.shape
    per_half = tokens // ROWS_STEP
    tiles = width // OUT_TILE
    bf16, f32 = jnp.bfloat16, jnp.float32
    dma = pltpu.SemaphoreType.DMA
    vmem = pl.BlockSpec(memory_space=pltpu.VMEM)
    smem = pl.BlockSpec(memory_space=pltpu.SMEM)
    hbm = pl.BlockSpec(memory_space=pl.ANY)
    return pl.pallas_call(
        functools.partial(layer_kernel, n, bits),
        out_shape=jax.ShapeDtypeStruct((tok, width), bf16),
        in_specs=[smem, vmem, vmem, hbm, hbm, vmem, vmem, vmem, vmem, hbm, hbm],
        out_specs=vmem,
        scratch_shapes=[
            pltpu.VMEM((halves, per_half, ROWS_STEP) + cache.shape[2:], bf16),
            pltpu.VMEM(wo.shape, bf16),
            pltpu.VMEM(gate_up.shape[1:], bf16),
            pltpu.VMEM(down.shape[1:], bf16),
            pltpu.VMEM((halves, tokens, q_width // HEAD_SIZE, HEAD_SIZE), f32),
            pltpu.VMEM((halves * per_half, ROWS_STEP, q_width), f32),
            pltpu.VMEM((tiles, halves, tokens, OUT_TILE), f32),
            pltpu.VMEM((tiles, tok, OUT_TILE), f32),
            pltpu.VMEM((tok, width), f32),
            [
                pltpu.VMEM((2, n, tok, width // 2), bf16),
                pltpu.VMEM((2, n, tok, width // 2 + extra), bf16),
            ],
            pltpu.VMEM((2, size, tok, down.shape[1]), bf16),
            pltpu.VMEM((2, n, tok, width), bf16),
            pltpu.VMEM((n, tok, width), bf16),
            pltpu.VMEM((n, tok, width), bf16),
            dma((halves, per_half)),
            dma((3,)),
            dma((tiles,)),
            dma((tiles,)),
        ]
        + [dma((2, n))] * 4
        + [dma((n,))] * 4,
        compiler_params=pltpu.CompilerParams(
            collective_id=0, has_side_effects=True, vmem_limit_bytes=VMEM_LIMIT
        ),
        name="layer",
    )(lens, queries, latest, cache, wo, residual, gain, router, routes, gate_up, down)


def solution(mesh):
    n = mesh.shape["dev"]

    def per_device(
        residual_in,
        queries,
        latest_key_value,
        key_value_cache,
        cache_len,
        out_weight,
        norm_gain,
        router_weight,
        routes,
        expert_gate_up,
        expert_down,
    ):
        return layer(
            n,
            cache_len,
            queries,
            latest_key_value,
            key_value_cache,
            out_weight,
            residual_in,
            norm_gain,
            router_weight.T,
            routes.T,
            expert_gate_up,
            expert_down,
        )

    placed = (
        P(("grp", "dev"), None),
        P(None, "dev", "grp"),
        P(None, "dev", "grp", None),
        P(None, "dev", "grp", None, None),
        P(None, "dev"),
        P("grp", None),
        P(),
        P(),
        P(("grp", "dev"), None),
        P(("grp", "dev"), None, None),
        P(("grp", "dev"), None, None),
    )
    return jax.shard_map(
        per_device, mesh=mesh, in_specs=placed, out_specs=P(("grp", "dev"), None), check_vma=False
    )
```

```python
import functools
import math

import jax
import jax.numpy as jnp
from jax import lax
from jax.experimental import pallas as pl
from jax.experimental.pallas import tpu as pltpu
from jax.sharding import PartitionSpec as P

HEAD_SIZE = 128
MESH = pl.DeviceIdType.MESH
ROWS_STEP = 8
OUT_TILE = 512
VMEM_LIMIT = 60 * 1024 * 1024


def layer_kernel(
    n,
    bits,
    lens_ref,
    q_ref,
    new_ref,
    cache_hbm,
    wo_hbm,
    res_ref,
    gain_ref,
    router_ref,
    routes_ref,
    wgu_hbm,
    wd_hbm,
    out_ref,
    kv,
    wo,
    wgu,
    wd,
    qs,
    att,
    pout,
    xsib,
    hid,
    gath,
    act,
    part,
    rsib,
    racc,
    ksem,
    wsem,
    xsend,
    xrecv,
    gsend,
    grecv,
    ssend,
    srecv,
    bsend,
    brecv,
    rsend,
    rrecv,
):
    g = lax.axis_index("grp")
    d = lax.axis_index("dev")
    tok, width = res_ref.shape
    experts = router_ref.shape[0]
    ff = wd.shape[0]
    sib = (1 - g, d)
    halves, tokens = q_ref.shape[:2]
    per_half = tokens // ROWS_STEP
    steps = halves * per_half
    kv_heads, positions = cache_hbm.shape[2:4]
    q_heads = q_ref.shape[2] // HEAD_SIZE
    group = q_heads // kv_heads
    scale = 1.0 / math.sqrt(HEAD_SIZE)

    def load_kv(half, s):
        return pltpu.make_async_copy(
            cache_hbm.at[half, pl.ds(s * ROWS_STEP, ROWS_STEP)],
            kv.at[half, s],
            ksem.at[half, s],
        )

    load_o = pltpu.make_async_copy(wo_hbm, wo, wsem.at[0])
    load_gu = pltpu.make_async_copy(wgu_hbm.at[0], wgu, wsem.at[1])
    load_d = pltpu.make_async_copy(wd_hbm.at[0], wd, wsem.at[2])
    for half in range(halves):
        for s in range(per_half):
            load_kv(half, s).start()

    def peer(j):
        m = 1 << (bits - 1 - j)
        if bits >= 2 and j == bits - 2:
            m = 1 + g
        elif bits >= 2 and j == bits - 1:
            m = 2 - g
        return (g, d + m * (1 - 2 * ((d // m) % 2)))

    peers = [peer(j) for j in range(bits)]
    barrier = pltpu.get_barrier_semaphore()
    for target in peers + [sib]:
        pl.semaphore_signal(barrier, inc=1, device_id=target, device_id_type=MESH)

    def remote(src, dst, send, recv, target):
        return pltpu.make_async_remote_copy(
            src_ref=src,
            dst_ref=dst,
            send_sem=send,
            recv_sem=recv,
            device_id=target,
            device_id_type=MESH,
        )

    for half in range(halves):
        q = q_ref[half].astype(jnp.float32)
        q = jnp.stack([q[:, j * HEAD_SIZE : (j + 1) * HEAD_SIZE] for j in range(q_heads)], axis=0)
        qs[half] = jnp.swapaxes(q, 0, 1)

    pairs = [(r, h) for r in range(ROWS_STEP) for h in range(kv_heads)]

    def attend(i, carry):
        half = i // per_half
        s = i % per_half
        load_kv(half, s).wait()

        @pl.when(i == 0)
        def _():
            load_o.start()

        first = pl.multiple_of(s * ROWS_STEP, ROWS_STEP)
        q = qs[half, pl.ds(first, ROWS_STEP)].reshape(ROWS_STEP, kv_heads, group, HEAD_SIZE)
        new = new_ref[half, pl.ds(first, ROWS_STEP)].astype(jnp.float32)[:, :, None, :]
        own = jnp.exp(jnp.sum(q * new[..., :HEAD_SIZE], axis=-1, keepdims=True) * scale)
        qb = q.astype(jnp.bfloat16)
        place = lax.broadcasted_iota(jnp.int32, (group, positions), 1)
        lens = [lens_ref[half, first + r] for r in range(ROWS_STEP)]
        scores = [
            lax.dot_general(
                qb[r, h],
                kv[half, s, r, h, :, :HEAD_SIZE],
                (((1,), (1,)), ((), ())),
                preferred_element_type=jnp.float32,
            )
            for r, h in pairs
        ]
        raised = [
            jnp.where(place < lens[r], jnp.exp(x * scale), 0.0) for (r, h), x in zip(pairs, scores)
        ]
        inverse = [
            1.0 / (jnp.sum(e, axis=1, keepdims=True) + own[r, h]) for (r, h), e in zip(pairs, raised)
        ]
        weights = [(e * v).astype(jnp.bfloat16) for e, v in zip(raised, inverse)]
        mixed = [
            jnp.dot(w, kv[half, s, r, h, :, HEAD_SIZE:], preferred_element_type=jnp.float32)
            for (r, h), w in zip(pairs, weights)
        ]
        mixed = [
            o
            + (own[r, h] * v).astype(jnp.bfloat16).astype(jnp.float32) * new[r, h, :, HEAD_SIZE:]
            for (r, h), o, v in zip(pairs, mixed, inverse)
        ]
        mixed = jnp.stack(
            [
                jnp.concatenate(mixed[r * kv_heads : (r + 1) * kv_heads], axis=0)
                for r in range(ROWS_STEP)
            ],
            axis=0,
        )
        mixed = jnp.swapaxes(mixed, 0, 1)
        att[i] = jnp.concatenate([mixed[j] for j in range(q_heads)], axis=1)
        return carry

    lax.fori_loop(0, steps, attend, 0)
    load_gu.start()
    load_d.start()
    pl.semaphore_wait(barrier, bits + 1)
    load_o.wait()
    attended = att[...].reshape(halves * tokens, q_heads * HEAD_SIZE).astype(jnp.bfloat16)
    swaps = []
    for t in range(width // OUT_TILE):
        cols = slice(t * OUT_TILE, (t + 1) * OUT_TILE)
        y = jnp.dot(attended, wo[:, cols], preferred_element_type=jnp.float32)
        pout[t] = y.reshape(halves, tokens, OUT_TILE)
        swaps.append(remote(pout.at[t, 1 - g], xsib.at[t], xsend.at[t], xrecv.at[t], sib))
        swaps[-1].start()
    squares = jnp.zeros((tok, 1), jnp.float32)
    for t in range(width // OUT_TILE):
        cols = slice(t * OUT_TILE, (t + 1) * OUT_TILE)
        swaps[t].wait()
        h = res_ref[:, cols].astype(jnp.float32) + (pout[t, g] + xsib[t])
        hid[:, cols] = h
        squares = squares + jnp.sum(h * h, axis=-1, keepdims=True)
    inv_norm = lax.rsqrt(squares * (1.0 / width) + 1e-06)
    gain = gain_ref[...].astype(jnp.float32).reshape(1, width)
    normed = (hid[...] * inv_norm * gain).astype(jnp.bfloat16)
    logits = lax.dot_general(
        router_ref[...], normed, (((1,), (1,)), ((), ())), preferred_element_type=jnp.float32
    )
    name = lax.broadcasted_iota(jnp.int32, (experts, tok), 0)
    routes = routes_ref[...]
    routed = name == routes[0:1, :]
    for k in range(1, routes.shape[0]):
        routed = jnp.logical_or(routed, name == routes[k : k + 1, :])
    picked = jnp.where(routed, jnp.exp(logits), 0.0)
    gates = picked / jnp.sum(picked, axis=0, keepdims=True)
    extra = gath.shape[3] - width
    if extra > experts:
        gates = jnp.concatenate([gates, jnp.zeros((extra - experts, tok), jnp.float32)], axis=0)
    gates = jnp.concatenate([gates, jnp.zeros((extra, 128 - tok), jnp.float32)], axis=1)
    gath[0, 0, :, :width] = normed
    gath[0, 0, :, width:] = jnp.transpose(gates)[:tok].astype(jnp.bfloat16)

    sends = []

    def forward(slot):
        first = slot.bit_length()
        for j in range(first, bits):
            there = slot | (1 << j)
            sends.append(
                remote(gath.at[0, slot], gath.at[0, there], gsend.at[there], grecv.at[there], peers[j])
            )
            sends[-1].start()
        sends.append(remote(gath.at[0, slot], gath.at[1, slot], ssend.at[slot], srecv.at[slot], sib))
        sends[-1].start()

    def arrived(slot):
        remote(gath.at[0, slot], gath.at[0, slot], gsend.at[slot], grecv.at[slot], sib).wait_recv()

    def arrived_sib(slot):
        remote(gath.at[0, slot], gath.at[1, slot], ssend.at[slot], srecv.at[slot], sib).wait_recv()

    half = n // 2
    forward(0)
    for slot in range(1, half):
        arrived(slot)
        forward(slot)

    expert = g * n + d
    size = min(8, half)
    rows = 2 * size * tok

    def gate_up(base, t, tile):
        x = gath[:, pl.ds(base, size), :, :width].reshape(rows, width)
        gate = jnp.dot(x, wgu[:, t : t + tile], preferred_element_type=jnp.float32)
        up = jnp.dot(x, wgu[:, ff + t : ff + t + tile], preferred_element_type=jnp.float32)
        act[:, :, :, t : t + tile] = (
            (gate / (1.0 + jnp.exp(-gate)) * up).astype(jnp.bfloat16).reshape(2, size, tok, tile)
        )

    def down(base, start, count):
        span = slice(start, start + count)
        own_rows = 2 * count * tok
        weights = gath[:, base + start : base + start + count, :, width:]
        weights = weights.reshape(own_rows, extra).astype(jnp.float32)
        mine = lax.broadcasted_iota(jnp.int32, (own_rows, extra), 1) == expert
        weight = jnp.sum(jnp.where(mine, weights, 0.0), axis=1, keepdims=True)
        x = act[:, span].reshape(own_rows, ff)
        tile = 512
        for t in range(0, width, tile):
            y = jnp.dot(x, wd[:, t : t + tile], preferred_element_type=jnp.float32)
            y = (y * weight).astype(jnp.bfloat16).reshape(2, count, tok, tile)
            part[:, base + start : base + start + count, :, t : t + tile] = y

    FT = 256
    for slot in range(half):
        arrived_sib(slot)
    load_gu.wait()
    pending = list(range(half, n))
    tiles = list(range(0, ff, FT))
    for at in range(0, half, size):
        for t in tiles:
            gate_up(at, t, FT)
            if at == 0:
                count = -(-half // len(tiles))
                for slot in pending[:count]:
                    arrived(slot)
                    forward(slot)
                pending = pending[count:]
        if at == 0:
            load_d.wait()
        down(at, 0, size)

    def give(slot):
        sends.append(remote(part.at[1, slot], rsib.at[slot], bsend.at[slot], brecv.at[slot], sib))
        sends[-1].start()

    def add_to(slot, more):
        part[0, slot] = (part[0, slot].astype(jnp.float32) + more.astype(jnp.float32)).astype(
            jnp.bfloat16
        )

    def taken(slot):
        remote(part.at[1, slot], rsib.at[slot], bsend.at[slot], brecv.at[slot], sib).wait_recv()
        add_to(slot, rsib[slot])

    order = [bits - 2, bits - 1] + list(range(bits - 3, -1, -1)) if bits >= 2 else [0]
    first_bit = 1 << order[0]

    def ship(slot, step):
        sends.append(
            remote(
                part.at[0, slot],
                racc.at[slot],
                rsend.at[slot],
                rrecv.at[slot],
                peers[order[step]],
            )
        )
        sends[-1].start()

    def received(source):
        remote(part.at[0, 0], racc.at[source], rsend.at[source], rrecv.at[source], sib).wait_recv()

    def absorb(slot, step):
        source = slot | (1 << order[step])
        received(source)
        add_to(slot, racc[source])

    early = [s for s in range(half) if s & first_bit] + [s for s in range(half) if not s & first_bit]
    for slot in early:
        give(slot)
    for slot in range(half, n):
        arrived_sib(slot)
    waiting = list(early)
    for at in range(half, n, size):
        for t in tiles:
            gate_up(at, t, FT)
            if at == half:
                count = -(-half // len(tiles))
                for slot in waiting[:count]:
                    taken(slot)
                    if slot & first_bit:
                        ship(slot, 0)
                waiting = waiting[count:]
        down(at, 0, size)
        for slot in reversed(range(at, at + size)):
            give(slot)
    for slot in reversed(range(half, n)):
        taken(slot)
        if slot & first_bit:
            ship(slot, 0)

    live = [s for s in range(n) if not s & first_bit]
    for step in range(1, len(order)):
        out_going = [s for s in live if s & (1 << order[step])]
        staying = [s for s in live if not s & (1 << order[step])]
        for s in reversed(out_going):
            absorb(s, step - 1)
            ship(s, step)
        for s in reversed(staying):
            absorb(s, step - 1)
        live = staying
    source = 1 << order[-1]
    received(source)
    out_ref[...] = (
        hid[...] + (part[0, 0].astype(jnp.float32) + racc[source].astype(jnp.float32))
    ).astype(jnp.bfloat16)
    for copy in sends:
        copy.wait_send()


def layer(n, lens, queries, latest, cache, wo, residual, gain, router, routes, gate_up, down):
    tok, width = residual.shape
    bits = n.bit_length() - 1
    extra = -(-router.shape[0] // 128) * 128
    size = min(8, n // 2)
    halves, tokens, q_width = queries.shape
    per_half = tokens // ROWS_STEP
    tiles = width // OUT_TILE
    bf16, f32 = jnp.bfloat16, jnp.float32
    dma = pltpu.SemaphoreType.DMA
    vmem = pl.BlockSpec(memory_space=pltpu.VMEM)
    smem = pl.BlockSpec(memory_space=pltpu.SMEM)
    hbm = pl.BlockSpec(memory_space=pl.ANY)
    return pl.pallas_call(
        functools.partial(layer_kernel, n, bits),
        out_shape=jax.ShapeDtypeStruct((tok, width), bf16),
        in_specs=[smem, vmem, vmem, hbm, hbm, vmem, vmem, vmem, vmem, hbm, hbm],
        out_specs=vmem,
        scratch_shapes=[
            pltpu.VMEM((halves, per_half, ROWS_STEP) + cache.shape[2:], bf16),
            pltpu.VMEM(wo.shape, bf16),
            pltpu.VMEM(gate_up.shape[1:], bf16),
            pltpu.VMEM(down.shape[1:], bf16),
            pltpu.VMEM((halves, tokens, q_width // HEAD_SIZE, HEAD_SIZE), f32),
            pltpu.VMEM((halves * per_half, ROWS_STEP, q_width), f32),
            pltpu.VMEM((tiles, halves, tokens, OUT_TILE), f32),
            pltpu.VMEM((tiles, tok, OUT_TILE), f32),
            pltpu.VMEM((tok, width), f32),
            pltpu.VMEM((2, n, tok, width + extra), bf16),
            pltpu.VMEM((2, size, tok, down.shape[1]), bf16),
            pltpu.VMEM((2, n, tok, width), bf16),
            pltpu.VMEM((n, tok, width), bf16),
            pltpu.VMEM((n, tok, width), bf16),
            dma((halves, per_half)),
            dma((3,)),
            dma((tiles,)),
            dma((tiles,)),
        ]
        + [dma((n,))] * 8,
        compiler_params=pltpu.CompilerParams(
            collective_id=0, has_side_effects=True, vmem_limit_bytes=VMEM_LIMIT
        ),
        name="layer",
    )(lens, queries, latest, cache, wo, residual, gain, router, routes, gate_up, down)


def solution(mesh):
    n = mesh.shape["dev"]

    def per_device(
        residual_in,
        queries,
        latest_key_value,
        key_value_cache,
        cache_len,
        out_weight,
        norm_gain,
        router_weight,
        routes,
        expert_gate_up,
        expert_down,
    ):
        return layer(
            n,
            cache_len,
            queries,
            latest_key_value,
            key_value_cache,
            out_weight,
            residual_in,
            norm_gain,
            router_weight.T,
            routes.T,
            expert_gate_up,
            expert_down,
        )

    placed = (
        P(("grp", "dev"), None),
        P(None, "dev", "grp"),
        P(None, "dev", "grp", None),
        P(None, "dev", "grp", None, None),
        P(None, "dev"),
        P("grp", None),
        P(),
        P(),
        P(("grp", "dev"), None),
        P(("grp", "dev"), None, None),
        P(("grp", "dev"), None, None),
    )
    return jax.shard_map(
        per_device, mesh=mesh, in_specs=placed, out_specs=P(("grp", "dev"), None), check_vma=False
    )
```
